512 devices in a mesh: seq: 256 (over z, x, y_lo, core), head: 2 (over y_hi).
Axes of the slice: x: 4, y: 8 (y_hi: 2, y_lo: 4; y = y_hi * 4 + y_lo), z: 8, core: 2. Of those that a mesh axis runs over, the one named last changes fastest.
Arguments:
- queries: bfloat16 [65536, 2048], P('seq', 'head'), may hold values from -5 to 5
- key_vectors: bfloat16 [65536, 2048], P('seq', 'head'), may hold values from -5 to 5
- value_vectors: bfloat16 [65536, 2048], P('seq', 'head'), may hold values from -6 to 6
- norm_gain: float32 [2048], P('head'), may hold values from 0.5 to 1.5
- cotangent: bfloat16 [65536, 2048], P('seq', 'head'), may hold values from -6 to 6
Outputs:
- normed: bfloat16 [65536, 2048], P('seq', 'head')
- query_grad: bfloat16 [65536, 2048], P('seq', 'head')
- key_grad: bfloat16 [65536, 2048], P('seq', 'head')
- value_grad: bfloat16 [65536, 2048], P('seq', 'head')
The draws below stay inside these ranges and needn't reach their ends.
All inputs are finite; a program needn't handle non-finite values.
Results may differ from the reference program's by a relative error of at most 0.008.
Values may be sent and summed in bfloat16 or wider, within the bound.
No kernel may reach another device: no remote copies, remote signals or barrier semaphores. Data moves between devices by JAX's collectives and lax.ppermute only.
A program may use at most 64 MiB of HBM per device.

```python
from functools import partial
import jax
import jax.numpy as jnp
from jax import lax

HEADS = 16
HDIM = 128
BLOCK = 16
TOK_DEV = 256
TOKENS = 65536


def draw_queries(key, part):
    key = jax.random.fold_in(key, 1)
    shape = (TOKENS, HEADS * HDIM)
    values = jax.random.truncated_normal(key, -5.0, 5.0, shape)
    return values.astype(jnp.bfloat16)


def draw_key_vectors(key, part):
    key = jax.random.fold_in(key, 2)
    shape = (TOKENS, HEADS * HDIM)
    values = jax.random.truncated_normal(key, -5.0, 5.0, shape)
    return values.astype(jnp.bfloat16)


def shard_levels(rng, shape, split, smallest, top_value):
    factor_of, own = 1.0, jax.random.fold_in(rng, 6)
    for axis_at, parts in split:
        heights = jnp.exp(jax.random.uniform(jax.random.fold_in(own, axis_at), (parts,), jnp.float32, smallest / len(split), top_value / len(split)))
        factor_of = factor_of * jnp.repeat(heights, shape[axis_at] // parts).reshape([-1 if axis == axis_at else 1 for axis in range(len(shape))])
    return factor_of


def centred(own_key, dims, deviation, reach, cuts=(), kind=jnp.bfloat16):
    drawn = deviation * jax.random.normal(own_key, dims, jnp.float32)
    if cuts:
        drawn = drawn * shard_levels(own_key, dims, cuts, -0.22, 0.18)
    return jnp.clip(drawn, -reach, reach).astype(kind)


def setup_inputs(seed: int = 0) -> dict:
    streams_of = jax.random.split(jax.random.key(seed), 6)
    return {
        "queries": draw_queries(jax.random.fold_in(streams_of[5], 71), 0),
        "key_vectors": draw_key_vectors(jax.random.fold_in(streams_of[5], 71), 0),
        "value_vectors": centred(streams_of[2], (TOKENS, HEADS * HDIM), 1.0, 6.0, ((0, 256), (1, 2))),
        "norm_gain": jnp.clip(1.0 + 0.1 * jax.random.normal(streams_of[3], (HEADS * HDIM,), jnp.float32), 0.5, 1.5),
        "cotangent": centred(streams_of[4], (TOKENS, HEADS * HDIM), 1.0, 6.0, ((0, 256), (1, 2))),
    }


def pool_rows(stacked, factor, weight):
    shaped = stacked.reshape(stacked.shape[0], stacked.shape[1] // factor, factor, stacked.shape[2])
    return (lax.optimization_barrier(jnp.sum(shaped, axis=2, dtype=jnp.float32)) * weight).astype(jnp.bfloat16)

def unpool(grads, factor):
    spread = jnp.broadcast_to(grads[:, :, None, :], (grads.shape[0], grads.shape[1], factor, grads.shape[2]))
    return spread.reshape(grads.shape[0], grads.shape[1] * factor, grads.shape[2])

def key_masks(start_row, row_count, seq_total, rim_rows):
    query_pos = start_row + jnp.arange(row_count, dtype=jnp.int32)
    raw_pos = start_row - rim_rows + jnp.arange(row_count + 2 * rim_rows, dtype=jnp.int32)
    near_ok = jnp.abs(raw_pos[None, :] // rim_rows - query_pos[:, None] // rim_rows) <= 1
    near_ok = near_ok & (raw_pos >= 0)[None, :] & (raw_pos < seq_total)[None, :]
    middle_pos = start_row // 4 - rim_rows + jnp.arange(row_count // 4 + 2 * rim_rows, dtype=jnp.int32)
    middle_gap = middle_pos[None, :] // rim_rows - query_pos[:, None] // (4 * rim_rows)
    middle_ok = (jnp.abs(middle_gap) == 1) & (middle_pos >= 0)[None, :] & (middle_pos < seq_total // 4)[None, :]
    coarse_pos = start_row // rim_rows - rim_rows + jnp.arange(row_count // rim_rows + 2 * rim_rows, dtype=jnp.int32)
    coarse_gap = coarse_pos[None, :] // rim_rows - query_pos[:, None] // (rim_rows * rim_rows)
    coarse_ok = (jnp.abs(coarse_gap) == 1) & (coarse_pos >= 0)[None, :] & (coarse_pos < seq_total // rim_rows)[None, :]
    return jnp.concatenate([near_ok, middle_ok, coarse_ok], axis=1)

def attend(queries, near_ext, middle_ext, coarse_ext, key_mask):
    key_rows = jnp.concatenate([near_ext[0], middle_ext[0], coarse_ext[0]], axis=0)
    value_rows = jnp.concatenate([near_ext[1], middle_ext[1], coarse_ext[1]], axis=0)
    head_count = queries.shape[1] // HDIM
    query_heads = queries.astype(jnp.float32).reshape(queries.shape[0], head_count, HDIM)
    key_heads = key_rows.astype(jnp.float32).reshape(key_rows.shape[0], head_count, HDIM)
    value_heads = value_rows.astype(jnp.float32).reshape(value_rows.shape[0], head_count, HDIM)
    scores = jnp.einsum('qhd,khd->hqk', query_heads, key_heads, precision=lax.Precision.HIGHEST) * HDIM ** (-0.5)
    scores = jnp.where(key_mask[None, :, :], scores, -1e+30)
    highest = lax.optimization_barrier(jnp.max(scores, axis=2, keepdims=True))
    lifted = jnp.exp(scores - highest)
    weights = lifted / lax.optimization_barrier(jnp.sum(lifted, axis=2, keepdims=True))
    rounded = lax.optimization_barrier(weights.astype(jnp.bfloat16)).astype(jnp.float32)
    mixed_heads = jnp.einsum('hqk,khd->qhd', rounded, value_heads, precision=lax.Precision.HIGHEST)
    return mixed_heads.reshape(queries.shape[0], head_count * HDIM)

def assemble(pieces, rim_rows):
    inner_rows = pieces[:, :, rim_rows:-rim_rows].astype(jnp.float32)
    lower_rim = pieces[:, :, :rim_rows].astype(jnp.float32)
    upper_rim = pieces[:, :, -rim_rows:].astype(jnp.float32)
    empty_rim = jnp.zeros_like(lower_rim[:1])
    from_above = jnp.concatenate([lower_rim[1:], empty_rim], axis=0)
    from_below = jnp.concatenate([empty_rim, upper_rim[:-1]], axis=0)
    span_rows = inner_rows.shape[2]
    inner_rows = inner_rows + jnp.pad(from_below, ((0, 0), (0, 0), (0, span_rows - rim_rows), (0, 0)))
    inner_rows = inner_rows + jnp.pad(from_above, ((0, 0), (0, 0), (span_rows - rim_rows, 0), (0, 0)))
    return inner_rows.transpose(1, 0, 2, 3).reshape(2, -1, inner_rows.shape[3])

def reference(queries, key_vectors, value_vectors, norm_gain, cotangent):
    row_count = TOK_DEV
    rim_rows = BLOCK
    seq_total = queries.shape[0]
    block_total = seq_total // row_count
    feat_all = HEADS * HDIM
    stacked = jnp.stack([key_vectors, value_vectors])
    edges = ((0, 0), (rim_rows, rim_rows), (0, 0))
    near_pad = jnp.pad(stacked, edges)
    middle_pad = jnp.pad(pool_rows(stacked, 4, 0.5), edges)
    coarse_pad = jnp.pad(pool_rows(stacked, rim_rows, 0.25), edges)

    def one_block(block_index):
        start_row = (block_index * row_count).astype(jnp.int32)
        near_ext = lax.dynamic_slice_in_dim(near_pad, start_row, row_count + 2 * rim_rows, 1)
        middle_ext = lax.dynamic_slice_in_dim(middle_pad, (start_row // 4).astype(jnp.int32), row_count // 4 + 2 * rim_rows, 1)
        coarse_ext = lax.dynamic_slice_in_dim(coarse_pad, (start_row // rim_rows).astype(jnp.int32), row_count // rim_rows + 2 * rim_rows, 1)
        query_block = lax.dynamic_slice_in_dim(queries, start_row, row_count, 0)
        cot_block = lax.dynamic_slice_in_dim(cotangent, start_row, row_count, 0)
        key_mask = key_masks(start_row, row_count, seq_total, rim_rows)
        attended, pullback = jax.vjp(partial(attend, key_mask=key_mask), query_block, near_ext, middle_ext, coarse_ext)
        scaled = cot_block.astype(jnp.float32) * norm_gain[None, :]
        squares = lax.optimization_barrier(jnp.sum(attended * attended, axis=1))
        crossed = lax.optimization_barrier(jnp.sum(scaled * attended, axis=1))
        factor = lax.rsqrt(squares / feat_all + 1e-06)
        normed = (norm_gain[None, :] * attended * factor[:, None]).astype(jnp.bfloat16)
        grad_out = factor[:, None] * scaled - attended * (factor * factor * factor * crossed / feat_all)[:, None]
        query_grad, near_grad, middle_grad, coarse_grad = pullback(grad_out)
        return (normed, query_grad, near_grad, middle_grad, coarse_grad)
    normed, query_grad, near_grad, middle_grad, coarse_grad = lax.map(one_block, jnp.arange(block_total, dtype=jnp.int32))
    total_grad = assemble(near_grad, rim_rows)
    total_grad = total_grad + unpool(assemble(middle_grad, rim_rows), 4) * 0.5
    total_grad = total_grad + unpool(assemble(coarse_grad, rim_rows), rim_rows) * 0.25
    return (normed.reshape(seq_total, feat_all), query_grad.reshape(seq_total, feat_all), total_grad[0].astype(jnp.bfloat16), total_grad[1].astype(jnp.bfloat16))
```

```python
from functools import partial

import jax
import jax.numpy as jnp
from jax import lax
from jax.experimental import pallas as pl
from jax.experimental.pallas import tpu as pltpu
from jax.sharding import PartitionSpec as P

HEADS = 16
HDIM = 128
BLOCK = 16
SCALE = HDIM**-0.5
F32 = jnp.float32
BF16 = jnp.bfloat16

SIDE = 3 * BLOCK
OWN_RAW = 9 * BLOCK
OWN_MID = 3 * BLOCK
OWN = OWN_RAW + OWN_MID
WINDOW = SIDE + OWN + BLOCK
GROUP = 128


def dot(a, b, ca, cb):
    return lax.dot_general(a, b, (((ca,), (cb,)), ((), ())), preferred_element_type=F32)


def head_cols(h):
    return pl.ds(h * HDIM, HDIM)


def pool_matrix(rows):
    shape = (rows // 4 + rows // 16, rows)
    out_row = lax.broadcasted_iota(jnp.int32, shape, 0)
    row = lax.broadcasted_iota(jnp.int32, shape, 1)
    middle = (row // 4 == out_row).astype(F32) * 0.5
    coarse = (row // 16 == out_row - rows // 4).astype(F32) * 0.25
    return jnp.where(out_row < rows // 4, middle, coarse).astype(BF16)


def pack_kernel(where_ref, k_ref, v_ref, far_ref, near_ref, mid_ref):
    rows = k_ref.shape[0]
    mids = rows // 4
    parity = where_ref[0] % 2
    pool = pool_matrix(rows)
    far_raw = pl.multiple_of(parity * (rows - BLOCK), BLOCK)
    near_raw = pl.multiple_of((1 - parity) * (rows - BLOCK), BLOCK)
    far_mid = pl.multiple_of(parity * (mids - BLOCK), BLOCK)
    near_mid = pl.multiple_of((1 - parity) * (mids - BLOCK), BLOCK)
    for i, ref in enumerate((k_ref, v_ref)):
        pooled = dot(pool, ref[...], 1, 0).astype(BF16)
        mid_ref[i] = pooled[:mids]
        base = i * SIDE
        for out_ref, raw_at, mid_at in ((far_ref, far_raw, far_mid), (near_ref, near_raw, near_mid)):
            out_ref[base : base + BLOCK] = ref[pl.ds(raw_at, BLOCK)]
            out_ref[base + BLOCK : base + 2 * BLOCK] = mid_ref[i, pl.ds(mid_at, BLOCK)]
            out_ref[base + 2 * BLOCK : base + 3 * BLOCK] = pooled[mids:]


def place_sides(parity, far_ref, near_ref, side_ref):
    @pl.when(parity == 0)
    def _():
        side_ref[0] = far_ref[...]
        side_ref[1] = near_ref[...]

    @pl.when(parity == 1)
    def _():
        side_ref[0] = near_ref[...]
        side_ref[1] = far_ref[...]


def window(i, g, cols, side_ref, raw_ref, mid_ref):
    raw_at, mid_at = (g * (raw_ref.shape[0] - OWN_RAW), g * (mid_ref.shape[1] - OWN_MID))
    base = i * SIDE
    return jnp.concatenate(
        [
            side_ref[g, base : base + SIDE, cols],
            raw_ref[raw_at : raw_at + OWN_RAW, cols],
            mid_ref[i, mid_at : mid_at + OWN_MID, cols],
            side_ref[1 - g, base + 2 * BLOCK : base + SIDE, cols],
        ],
        axis=0,
    )


def allowed(g, has_below, has_above):
    shape = (WINDOW, GROUP)
    kb = lax.broadcasted_iota(jnp.int32, shape, 0) // BLOCK
    qb = lax.broadcasted_iota(jnp.int32, shape, 1) // BLOCK
    qm = qb // 4
    raw_gap = kb - 3 - g - qb
    mid_gap = kb - 12 - g - qm
    edge_raw = qb == (7 if g else 0)
    edge_mid = qm == (1 if g else 0)
    one = jnp.ones(shape, jnp.int32)
    none = jnp.zeros(shape, jnp.int32)
    own = jnp.where(kb < 12, jnp.where(jnp.abs(raw_gap) <= 1, one, none), jnp.where(jnp.abs(mid_gap) == 1, one, none))
    side = jnp.where(kb == 0, jnp.where(edge_raw, one, none), jnp.where(kb == 1, jnp.where(edge_mid, one, none), one))
    valid_side, valid_other = (has_above, has_below) if g else (has_below, has_above)
    return jnp.where(kb < 3, side * valid_side, jnp.where(kb == 15, one * valid_other, own))


def forward_kernel(
    where_ref, q_ref, k_ref, v_ref, mid_ref, far_ref, near_ref, gain_ref, cot_ref, w_ref, att_ref, sums_ref, side_ref, bias_ref
):
    place_sides(where_ref[0] % 2, far_ref, near_ref, side_ref)
    for g in range(2):
        ok = allowed(g, where_ref[1], where_ref[2])
        bias_ref[g] = jnp.where(ok == 1, 0.0, -1e30)
    for g in range(2):
        rows = slice(g * GROUP, (g + 1) * GROUP)
        squares = jnp.zeros((GROUP, HDIM), F32)
        crossed = jnp.zeros((GROUP, HDIM), F32)
        for h in range(8):
            cols = slice(h * HDIM, (h + 1) * HDIM)
            keys = window(0, g, cols, side_ref, k_ref, mid_ref)
            values = window(1, g, cols, side_ref, v_ref, mid_ref)
            scores = dot(keys, q_ref[rows, cols], 1, 1) * SCALE + bias_ref[g]
            lifted = jnp.exp(scores - jnp.max(scores, axis=0, keepdims=True))
            weights = lifted * (1.0 / jnp.sum(lifted, axis=0, keepdims=True))
            w_ref[g, h] = weights
            mixed = dot(weights.astype(BF16), values, 0, 0)
            att_ref[rows, cols] = mixed
            squares += mixed * mixed
            crossed += mixed * (cot_ref[rows, cols].astype(F32) * gain_ref[:, cols])
        sums_ref[0:1, rows] = jnp.sum(squares.T, axis=0, keepdims=True)
        sums_ref[1:2, rows] = jnp.sum(crossed.T, axis=0, keepdims=True)


def row_factors(sums_ref, others_ref):
    feat_all = HEADS * HDIM
    totals = sums_ref[...] + others_ref[...]
    factor = lax.rsqrt(totals[0:1] / feat_all + 1e-06)
    cross = factor * factor * factor * totals[1:2] / feat_all
    both = jnp.concatenate([factor, cross, jnp.zeros((6, factor.shape[1]), F32)], axis=0)
    columns = both.T
    return columns[:, 0:1], columns[:, 1:2]


def pieces_kernel(
    where_ref, q_ref, v_ref, mid_ref, far_ref, near_ref, gain_ref, cot_ref, w_ref, att_ref, sums_ref, others_ref,
    far_out, near_out, ds_ref, dout_ref, side_ref, piece_ref,
):
    parity = where_ref[0] % 2
    place_sides(parity, far_ref, near_ref, side_ref)
    factor, cross = row_factors(sums_ref, others_ref)
    for h in range(8):
        cols = slice(h * HDIM, (h + 1) * HDIM)
        remote = []
        for g in range(2):
            rows = slice(g * GROUP, (g + 1) * GROUP)
            scaled = cot_ref[rows, cols].astype(F32) * gain_ref[:, cols]
            grad_out = (factor[rows] * scaled - cross[rows] * att_ref[rows, cols]).astype(BF16)
            dout_ref[rows, cols] = grad_out
            values = window(1, g, cols, side_ref, v_ref, mid_ref)
            grad_w = dot(values, grad_out, 1, 1)
            weights = w_ref[g, h]
            middle = jnp.sum(weights * grad_w, axis=0, keepdims=True)
            ds = (weights * (grad_w - middle) * SCALE).astype(BF16)
            ds_ref[g, h] = ds
            low = jnp.concatenate([weights[:SIDE], weights[SIDE + OWN :]], axis=0).astype(BF16)
            ds_rim = jnp.concatenate([ds[:SIDE], ds[SIDE + OWN :]], axis=0)
            remote.append((dot(ds_rim, q_ref[rows, cols], 1, 0), dot(low, grad_out, 1, 0)))
        for i in range(2):
            base = i * SIDE
            for g in range(2):
                mine, other = remote[g][i], remote[1 - g][i]
                piece_ref[g, base : base + 2 * BLOCK, cols] = mine[: 2 * BLOCK].astype(BF16)
                piece_ref[g, base + 2 * BLOCK : base + SIDE, cols] = (mine[2 * BLOCK : SIDE] + other[SIDE:]).astype(BF16)

    @pl.when(parity == 0)
    def _():
        far_out[...] = piece_ref[0]
        near_out[...] = piece_ref[1]

    @pl.when(parity == 1)
    def _():
        far_out[...] = piece_ref[1]
        near_out[...] = piece_ref[0]


def spread_matrix(rows, kinds):
    parts = []
    for first, factor, weight, count in kinds:
        row = lax.broadcasted_iota(jnp.int32, (rows, count), 0)
        at = lax.broadcasted_iota(jnp.int32, (rows, count), 1)
        parts.append((((row - first) // factor == at) & (row >= first)).astype(F32) * weight)
    return jnp.concatenate(parts, axis=1).astype(BF16)


def own_kernel(
    where_ref, q_ref, k_ref, mid_ref, far_ref, near_ref, gain_ref, w_ref, att_ref, sums_ref, others_ref, ds_ref, dout_ref,
    normed_ref, dq_ref, own_ref, side_ref,
):
    place_sides(where_ref[0] % 2, far_ref, near_ref, side_ref)
    factor, _ = row_factors(sums_ref, others_ref)
    rows_all = q_ref.shape[0]
    spread = spread_matrix(rows_all, [(0, 4, 0.5, rows_all // 4)])
    for h in range(8):
        cols = slice(h * HDIM, (h + 1) * HDIM)
        inner = []
        for g in range(2):
            rows = slice(g * GROUP, (g + 1) * GROUP)
            normed_ref[rows, cols] = (gain_ref[:, cols] * att_ref[rows, cols] * factor[rows]).astype(BF16)
            ds = ds_ref[g, h]
            keys = window(0, g, cols, side_ref, k_ref, mid_ref)
            dq_ref[rows, cols] = dot(ds, keys, 0, 0).astype(BF16)
            low = w_ref[g, h, SIDE : SIDE + OWN].astype(BF16)
            inner.append((dot(ds[SIDE : SIDE + OWN], q_ref[rows, cols], 1, 0), dot(low, dout_ref[rows, cols], 1, 0)))
        for i in range(2):
            lower, upper = inner[0][i], inner[1][i]
            both_raw = 2 * OWN_RAW - rows_all
            raw = jnp.concatenate(
                [lower[: OWN_RAW - both_raw], lower[OWN_RAW - both_raw : OWN_RAW] + upper[:both_raw], upper[both_raw:OWN_RAW]],
                axis=0,
            )
            low_mid, up_mid = lower[OWN_RAW:], upper[OWN_RAW:]
            both_mid = 2 * OWN_MID - rows_all // 4
            mid = jnp.concatenate(
                [low_mid[: OWN_MID - both_mid], low_mid[OWN_MID - both_mid :] + up_mid[:both_mid], up_mid[both_mid:]], axis=0
            ).astype(BF16)
            own_ref[i, :, cols] = raw + dot(spread, mid, 1, 0)


def final_kernel(where_ref, own_ref, far_ref, near_ref, dk_ref, dv_ref, side_ref):
    place_sides(where_ref[0] % 2, far_ref, near_ref, side_ref)
    rows = own_ref.shape[1]
    spread = [
        spread_matrix(rows, [(rows - BLOCK if g else 0, 1, 1.0, BLOCK), (rows - 4 * BLOCK if g else 0, 4, 0.5, BLOCK), (0, 16, 0.25, BLOCK)])
        for g in range(2)
    ]
    both = jnp.concatenate(spread, axis=1)
    for i, out_ref in enumerate((dk_ref, dv_ref)):
        got = jnp.concatenate([side_ref[0, i * SIDE : (i + 1) * SIDE], side_ref[1, i * SIDE : (i + 1) * SIDE]], axis=0)
        out_ref[...] = (own_ref[i] + dot(both, got, 1, 0)).astype(BF16)


def call(kernel, outs, scratch, flops, args):
    smem = pl.BlockSpec(memory_space=pltpu.SMEM)
    vmem = pl.BlockSpec(memory_space=pltpu.VMEM)
    return pl.pallas_call(
        kernel,
        out_shape=outs,
        in_specs=[smem] + [vmem] * (len(args) - 1),
        out_specs=jax.tree.map(lambda _: vmem, outs),
        scratch_shapes=scratch,
        compiler_params=pltpu.CompilerParams(vmem_limit_bytes=24 * 2**20),
        cost_estimate=pl.CostEstimate(flops=flops, bytes_accessed=4 * 2**20, transcendentals=0),
    )(*args)


def exchange(far, near):
    size = lax.axis_size("seq")
    far_pairs = [(i, i + 1) for i in range(1, size - 1, 2)]
    near_pairs = [(i, i + 1) for i in range(0, size, 2)]
    far_got = lax.ppermute(far, "seq", far_pairs + [(j, i) for i, j in far_pairs])
    near_got = lax.ppermute(near, "seq", near_pairs + [(j, i) for i, j in near_pairs])
    return far_got, near_got


def local(queries, key_vectors, value_vectors, norm_gain, cotangent):
    rows, feats = queries.shape
    index = lax.axis_index("seq").astype(jnp.int32)
    size = lax.axis_size("seq")
    where = jnp.stack([index, (index > 0).astype(jnp.int32), (index < size - 1).astype(jnp.int32)])
    gain = norm_gain.reshape(1, feats)
    heads = feats // HDIM
    arr = jax.ShapeDtypeStruct
    rim = arr((2 * SIDE, feats), BF16)
    sides = pltpu.VMEM((2, 2 * SIDE, feats), BF16)
    far, near, mid = call(
        pack_kernel, (rim, rim, arr((2, rows // 4, feats), BF16)), [], 10**8, (where, key_vectors, value_vectors)
    )
    far, near = exchange(far, near)
    weights, attended, sums = call(
        forward_kernel,
        (arr((2, heads, WINDOW, GROUP), F32), arr((rows, feats), F32), arr((2, rows), F32)),
        [sides, pltpu.VMEM((2, WINDOW, GROUP), F32)],
        10**9,
        (where, queries, key_vectors, value_vectors, mid, far, near, gain, cotangent),
    )
    others = lax.ppermute(sums, "head", [(0, 1), (1, 0)])
    far_piece, near_piece, ds, dout = call(
        pieces_kernel,
        (rim, rim, arr((2, heads, WINDOW, GROUP), BF16), arr((rows, feats), BF16)),
        [sides, sides],
        10**9,
        (where, queries, value_vectors, mid, far, near, gain, cotangent, weights, attended, sums, others),
    )
    far_got, near_got = exchange(far_piece, near_piece)
    normed, query_grad, own = call(
        own_kernel,
        (arr((rows, feats), BF16), arr((rows, feats), BF16), arr((2, rows, feats), F32)),
        [sides],
        10**9,
        (where, queries, key_vectors, mid, far, near, gain, weights, attended, sums, others, ds, dout),
    )
    key_grad, value_grad = call(
        final_kernel, (arr((rows, feats), BF16), arr((rows, feats), BF16)), [sides], 10**8, (where, own, far_got, near_got)
    )
    return normed, query_grad, key_grad, value_grad


def solution(mesh):
    in_specs = (P("seq", "head"), P("seq", "head"), P("seq", "head"), P("head"), P("seq", "head"))
    out_specs = (P("seq", "head"), P("seq", "head"), P("seq", "head"), P("seq", "head"))
    return jax.shard_map(local, mesh=mesh, in_specs=in_specs, out_specs=out_specs, check_vma=False)
```

```python
from functools import partial

import jax
import jax.numpy as jnp
from jax import lax
from jax.experimental import pallas as pl
from jax.experimental.pallas import tpu as pltpu
from jax.sharding import PartitionSpec as P

HEADS = 16
HDIM = 128
BLOCK = 16
SCALE = HDIM**-0.5
F32 = jnp.float32
BF16 = jnp.bfloat16

SIDE = 3 * BLOCK
OWN_RAW = 9 * BLOCK
OWN_MID = 3 * BLOCK
OWN = OWN_RAW + OWN_MID
WINDOW = SIDE + OWN + BLOCK
GROUP = 128


def dot(a, b, ca, cb):
    return lax.dot_general(a, b, (((ca,), (cb,)), ((), ())), preferred_element_type=F32)


def pool_matrix(rows):
    shape = (rows // 4 + rows // 16, rows)
    out_row = lax.broadcasted_iota(jnp.int32, shape, 0)
    row = lax.broadcasted_iota(jnp.int32, shape, 1)
    middle = (row // 4 == out_row).astype(F32) * 0.5
    coarse = (row // 16 == out_row - rows // 4).astype(F32) * 0.25
    return jnp.where(out_row < rows // 4, middle, coarse).astype(BF16)


def pack_side(i, k_or_v, upper, mid_ref, coarse_ref, out_ref):
    raw_at = pl.multiple_of(upper * (k_or_v.shape[0] - BLOCK), BLOCK)
    mid_at = pl.multiple_of(upper * (mid_ref.shape[1] - BLOCK), BLOCK)
    base = i * SIDE
    out_ref[base : base + BLOCK] = k_or_v[pl.ds(raw_at, BLOCK)]
    out_ref[base + BLOCK : base + 2 * BLOCK] = mid_ref[i, pl.ds(mid_at, BLOCK)]
    out_ref[base + 2 * BLOCK : base + 3 * BLOCK] = coarse_ref[i]


def pack_kernel(
    where_ref, k_hbm, v_hbm, q_hbm, cot_hbm, gain_hbm,
    k_ref, v_ref, q_ref, cot_ref, gain_ref, far_ref, mid_ref, coarse_ref, sems,
):
    copies = [
        pltpu.make_async_copy(src, dst, sems.at[n])
        for n, (src, dst) in enumerate(
            [(k_hbm, k_ref), (v_hbm, v_ref), (q_hbm, q_ref), (cot_hbm, cot_ref), (gain_hbm, gain_ref)]
        )
    ]
    for copy in copies:
        copy.start()
    rows = k_ref.shape[0]
    mids = rows // 4
    upper = where_ref[0] % 2
    pool = pool_matrix(rows)
    for i, ref in enumerate((k_ref, v_ref)):
        copies[i].wait()
        pooled = dot(pool, ref[...], 1, 0).astype(BF16)
        mid_ref[i] = pooled[:mids]
        coarse_ref[i] = pooled[mids:]
        pack_side(i, ref, upper, mid_ref, coarse_ref, far_ref)
    for copy in copies[2:]:
        copy.wait()


def place_sides(parity, far_ref, near_ref, side_ref):
    @pl.when(parity == 0)
    def _():
        side_ref[0] = far_ref[...]
        side_ref[1] = near_ref[...]

    @pl.when(parity == 1)
    def _():
        side_ref[0] = near_ref[...]
        side_ref[1] = far_ref[...]


def own_rows(i, g, cols, raw_ref, mid_ref):
    raw_at, mid_at = (g * (raw_ref.shape[0] - OWN_RAW), g * (mid_ref.shape[1] - OWN_MID))
    return [raw_ref[raw_at : raw_at + OWN_RAW, cols], mid_ref[i, mid_at : mid_at + OWN_MID, cols]]


def side_rows(i, g, cols, side_ref):
    base = i * SIDE
    return [side_ref[g, base : base + SIDE, cols], side_ref[1 - g, base + 2 * BLOCK : base + SIDE, cols]]


def window(i, g, cols, side_ref, raw_ref, mid_ref):
    mine, other = side_rows(i, g, cols, side_ref)
    return jnp.concatenate([mine, *own_rows(i, g, cols, raw_ref, mid_ref), other], axis=0)


def allowed(g, has_below, has_above):
    shape = (WINDOW, GROUP)
    kb = lax.broadcasted_iota(jnp.int32, shape, 0) // BLOCK
    qb = lax.broadcasted_iota(jnp.int32, shape, 1) // BLOCK
    qm = qb // 4
    raw_gap = kb - 3 - g - qb
    mid_gap = kb - 12 - g - qm
    edge_raw = qb == (7 if g else 0)
    edge_mid = qm == (1 if g else 0)
    one = jnp.ones(shape, jnp.int32)
    none = jnp.zeros(shape, jnp.int32)
    own = jnp.where(kb < 12, jnp.where(jnp.abs(raw_gap) <= 1, one, none), jnp.where(jnp.abs(mid_gap) == 1, one, none))
    side = jnp.where(kb == 0, jnp.where(edge_raw, one, none), jnp.where(kb == 1, jnp.where(edge_mid, one, none), one))
    valid_side, valid_other = (has_above, has_below) if g else (has_below, has_above)
    return jnp.where(kb < 3, side * valid_side, jnp.where(kb == 15, one * valid_other, own))


def local_kernel(
    where_ref, q_ref, k_ref, v_ref, mid_ref, coarse_ref, near_ref, lifted_ref, stats_ref, bias_ref
):
    for i, ref in enumerate((k_ref, v_ref)):
        pack_side(i, ref, 1 - where_ref[0] % 2, mid_ref, coarse_ref, near_ref)
    heads = lifted_ref.shape[1]
    for g in range(2):
        bias_ref[...] = jnp.where(allowed(g, 1, 1)[SIDE : SIDE + OWN] == 1, 0.0, -1e30)
        rows = slice(g * GROUP, (g + 1) * GROUP)
        for h in range(heads):
            cols = slice(h * HDIM, (h + 1) * HDIM)
            keys = jnp.concatenate(own_rows(0, g, cols, k_ref, mid_ref), axis=0)
            scores = dot(keys, q_ref[rows, cols], 1, 1) * SCALE + bias_ref[...]
            highest = jnp.max(scores, axis=0, keepdims=True)
            lifted = jnp.exp(scores - highest)
            lifted_ref[g, h] = lifted
            stats_ref[g, h : h + 1] = highest
            stats_ref[g, heads + h : heads + h + 1] = jnp.sum(lifted, axis=0, keepdims=True)


def forward_kernel(
    where_ref, q_ref, v_ref, mid_ref, far_ref, near_ref, gain_ref, cot_ref, lifted_ref, stats_ref,
    w_ref, att_ref, sums_ref, side_ref, bias_ref, side_lifted, side_stats,
):
    place_sides(where_ref[0] % 2, far_ref, near_ref, side_ref)
    heads = lifted_ref.shape[1]
    for g in range(2):
        ok = allowed(g, where_ref[1], where_ref[2])
        bias_ref[g] = jnp.where(jnp.concatenate([ok[:SIDE], ok[SIDE + OWN :]], axis=0) == 1, 0.0, -1e30)
    for g in range(2):
        rows = slice(g * GROUP, (g + 1) * GROUP)
        for h in range(heads):
            cols = slice(h * HDIM, (h + 1) * HDIM)
            keys = jnp.concatenate(side_rows(0, g, cols, side_ref), axis=0)
            scores = dot(keys, q_ref[rows, cols], 1, 1) * SCALE + bias_ref[g]
            highest = jnp.max(scores, axis=0, keepdims=True)
            lifted = jnp.exp(scores - highest)
            side_lifted[g, h] = lifted
            side_stats[g, h : h + 1] = highest
            side_stats[g, heads + h : heads + h + 1] = jnp.sum(lifted, axis=0, keepdims=True)
    for g in range(2):
        rows = slice(g * GROUP, (g + 1) * GROUP)
        own_high, side_high = stats_ref[g, :heads], side_stats[g, :heads]
        highest = jnp.maximum(own_high, side_high)
        own_part, side_part = jnp.exp(own_high - highest), jnp.exp(side_high - highest)
        inverse = 1.0 / (stats_ref[g, heads:] * own_part + side_stats[g, heads:] * side_part)
        own_part, side_part = own_part * inverse, side_part * inverse
        squares = jnp.zeros((GROUP, HDIM), F32)
        crossed = jnp.zeros((GROUP, HDIM), F32)
        for h in range(heads):
            cols = slice(h * HDIM, (h + 1) * HDIM)
            side_w = side_lifted[g, h] * side_part[h : h + 1]
            own_w = lifted_ref[g, h] * own_part[h : h + 1]
            weights = jnp.concatenate([side_w[:SIDE], own_w, side_w[SIDE:]], axis=0)
            w_ref[g, h] = weights
            mixed = dot(weights.astype(BF16), window(1, g, cols, side_ref, v_ref, mid_ref), 0, 0)
            att_ref[rows, cols] = mixed
            squares += mixed * mixed
            crossed += mixed * (cot_ref[rows, cols].astype(F32) * gain_ref[:, cols])
        sums_ref[0:1, rows] = jnp.sum(squares.T, axis=0, keepdims=True)
        sums_ref[1:2, rows] = jnp.sum(crossed.T, axis=0, keepdims=True)


def row_factors(sums_ref):
    feat_all = HEADS * HDIM
    totals = sums_ref[0] + sums_ref[1]
    factor = lax.rsqrt(totals[0:1] / feat_all + 1e-06)
    cross = factor * factor * factor * totals[1:2] / feat_all
    both = jnp.concatenate([factor, cross, jnp.zeros((6, factor.shape[1]), F32)], axis=0)
    columns = both.T
    return columns[:, 0:1], columns[:, 1:2]


def side_piece(g, q_ref, w_ref, ds_ref, dout_ref, out_ref):
    half = q_ref.shape[0] // 2
    mine = pl.ds(pl.multiple_of(g * half, half), half)
    other = pl.ds(pl.multiple_of((1 - g) * half, half), half)
    blank = jnp.zeros((2 * BLOCK, GROUP), BF16)
    for h in range(w_ref.shape[1]):
        cols = slice(h * HDIM, (h + 1) * HDIM)
        for i, (left, right) in enumerate(((ds_ref, q_ref), (w_ref, dout_ref))):
            far_part = jnp.concatenate([blank, left[1 - g, h, SIDE + OWN :].astype(BF16)], axis=0)
            lhs = jnp.concatenate([left[g, h, :SIDE].astype(BF16), far_part], axis=1)
            rhs = jnp.concatenate([right[mine, cols], right[other, cols]], axis=0)
            out_ref[i * SIDE : (i + 1) * SIDE, cols] = dot(lhs, rhs, 1, 0).astype(BF16)


def pieces_kernel(
    where_ref, q_ref, v_ref, mid_ref, side_ref, gain_ref, cot_ref, w_ref, att_ref, sums_ref,
    far_out, near_out, ds_ref, dout_ref,
):
    factor, cross = row_factors(sums_ref)
    for h in range(w_ref.shape[1]):
        cols = slice(h * HDIM, (h + 1) * HDIM)
        for g in range(2):
            rows = slice(g * GROUP, (g + 1) * GROUP)
            scaled = cot_ref[rows, cols].astype(F32) * gain_ref[:, cols]
            grad_out = (factor[rows] * scaled - cross[rows] * att_ref[rows, cols]).astype(BF16)
            dout_ref[rows, cols] = grad_out
            grad_w = dot(window(1, g, cols, side_ref, v_ref, mid_ref), grad_out, 1, 1)
            weights = w_ref[g, h]
            middle = jnp.sum(weights * grad_w, axis=0, keepdims=True)
            ds_ref[g, h] = (weights * (grad_w - middle) * SCALE).astype(BF16)
    side_piece(where_ref[0] % 2, q_ref, w_ref, ds_ref, dout_ref, far_out)
    side_piece(1 - where_ref[0] % 2, q_ref, w_ref, ds_ref, dout_ref, near_out)


def spread_matrix(rows, kinds):
    parts = []
    for first, factor, weight, count in kinds:
        row = lax.broadcasted_iota(jnp.int32, (rows, count), 0)
        at = lax.broadcasted_iota(jnp.int32, (rows, count), 1)
        parts.append((((row - first) // factor == at) & (row >= first)).astype(F32) * weight)
    return jnp.concatenate(parts, axis=1).astype(BF16)


def own_kernel(
    where_ref, q_ref, k_ref, mid_ref, side_ref, gain_ref, w_ref, att_ref, sums_ref, ds_ref, dout_ref,
    own_ref, normed_hbm, dq_hbm, normed_ref, dq_ref, sems,
):
    rows_all, feats = q_ref.shape
    factor, _ = row_factors(sums_ref)
    normed_ref[...] = (gain_ref[...] * att_ref[...] * factor).astype(BF16)
    copies = [pltpu.make_async_copy(normed_ref, normed_hbm, sems.at[0])]
    copies[0].start()
    spread = spread_matrix(rows_all, [(0, 4, 0.5, rows_all // 4)])
    heads = w_ref.shape[1]
    for h in range(heads):
        cols = slice(h * HDIM, (h + 1) * HDIM)
        inner = []
        for g in range(2):
            rows = slice(g * GROUP, (g + 1) * GROUP)
            ds = ds_ref[g, h]
            keys = window(0, g, cols, side_ref, k_ref, mid_ref)
            dq_ref[rows, cols] = dot(ds, keys, 0, 0).astype(BF16)
            low = w_ref[g, h, SIDE : SIDE + OWN].astype(BF16)
            inner.append((dot(ds[SIDE : SIDE + OWN], q_ref[rows, cols], 1, 0), dot(low, dout_ref[rows, cols], 1, 0)))
        if h % (heads // 2) == heads // 2 - 1:
            done = pl.ds((h + 1 - heads // 2) * HDIM, heads // 2 * HDIM)
            copies.append(pltpu.make_async_copy(dq_ref.at[:, done], dq_hbm.at[:, done], sems.at[len(copies)]))
            copies[-1].start()
        for i in range(2):
            lower, upper = inner[0][i], inner[1][i]
            both_raw = 2 * OWN_RAW - rows_all
            raw = jnp.concatenate(
                [lower[: OWN_RAW - both_raw], lower[OWN_RAW - both_raw : OWN_RAW] + upper[:both_raw], upper[both_raw:OWN_RAW]],
                axis=0,
            )
            low_mid, up_mid = lower[OWN_RAW:], upper[OWN_RAW:]
            both_mid = 2 * OWN_MID - rows_all // 4
            mid = jnp.concatenate(
                [low_mid[: OWN_MID - both_mid], low_mid[OWN_MID - both_mid :] + up_mid[:both_mid], up_mid[both_mid:]], axis=0
            ).astype(BF16)
            own_ref[i, :, cols] = raw + dot(spread, mid, 1, 0)
    for copy in copies:
        copy.wait()


def final_kernel(where_ref, own_ref, far_ref, near_ref, dk_hbm, dv_hbm, dk_ref, dv_ref, side_ref, sems):
    place_sides(where_ref[0] % 2, far_ref, near_ref, side_ref)
    rows = own_ref.shape[1]
    spread = [
        spread_matrix(rows, [(rows - BLOCK if g else 0, 1, 1.0, BLOCK), (rows - 4 * BLOCK if g else 0, 4, 0.5, BLOCK), (0, 16, 0.25, BLOCK)])
        for g in range(2)
    ]
    both = jnp.concatenate(spread, axis=1)
    copies = []
    for i, (out_ref, hbm) in enumerate(((dk_ref, dk_hbm), (dv_ref, dv_hbm))):
        got = jnp.concatenate([side_ref[0, i * SIDE : (i + 1) * SIDE], side_ref[1, i * SIDE : (i + 1) * SIDE]], axis=0)
        for part in range(2):
            at = slice(part * (rows // 2), (part + 1) * (rows // 2))
            out_ref[at] = (own_ref[i, at] + dot(both[at], got, 1, 0)).astype(BF16)
            copies.append(pltpu.make_async_copy(out_ref.at[at], hbm.at[at], sems.at[len(copies)]))
            copies[-1].start()
    for copy in copies:
        copy.wait()


SMEM = pl.BlockSpec(memory_space=pltpu.SMEM)
VMEM = pl.BlockSpec(memory_space=pltpu.VMEM)
HBM = pl.BlockSpec(memory_space=pltpu.HBM)


def call(kernel, args, in_specs, outs, out_specs, scratch, flops):
    return pl.pallas_call(
        kernel,
        out_shape=outs,
        in_specs=[SMEM, *in_specs],
        out_specs=out_specs,
        scratch_shapes=scratch,
        compiler_params=pltpu.CompilerParams(vmem_limit_bytes=24 * 2**20),
        cost_estimate=pl.CostEstimate(flops=flops, bytes_accessed=4 * 2**20, transcendentals=0),
    )(*args)


def far_swap(x):
    pairs = [(i, i + 1) for i in range(1, lax.axis_size("seq") - 1, 2)]
    return lax.ppermute(x, "seq", pairs + [(j, i) for i, j in pairs])


def near_swap(x):
    pairs = [(i, i + 1) for i in range(0, lax.axis_size("seq"), 2)]
    return lax.ppermute(x, "seq", pairs + [(j, i) for i, j in pairs])


def local(queries, key_vectors, value_vectors, norm_gain, cotangent):
    rows, feats = queries.shape
    index = lax.axis_index("seq").astype(jnp.int32)
    size = lax.axis_size("seq")
    where = jnp.stack([index, (index > 0).astype(jnp.int32), (index < size - 1).astype(jnp.int32)])
    heads = feats // HDIM
    inputs = (key_vectors, value_vectors, queries, cotangent, norm_gain.reshape(1, feats))
    arr = jax.ShapeDtypeStruct
    dma = pltpu.SemaphoreType.DMA
    whole = arr((rows, feats), BF16)
    rim = arr((2 * SIDE, feats), BF16)
    k, v, q, cot, gain, far, mid, coarse = call(
        pack_kernel,
        (where, *(pltpu.with_memory_space_constraint(x, pltpu.HBM) for x in inputs)),
        [HBM] * 5,
        (whole, whole, whole, whole, arr((1, feats), F32), rim, arr((2, rows // 4, feats), BF16), arr((2, BLOCK, feats), BF16)),
        (VMEM,) * 8,
        [dma((5,))],
        10**8,
    )
    far_got = far_swap(far)
    near, lifted, stats = call(
        local_kernel,
        (where, q, k, v, mid, coarse),
        [VMEM] * 5,
        (rim, arr((2, heads, OWN, GROUP), F32), arr((2, 2 * heads, GROUP), F32)),
        (VMEM,) * 3,
        [pltpu.VMEM((OWN, GROUP), F32)],
        10**9,
    )
    near_got = near_swap(near)
    weights, attended, sums, side = call(
        forward_kernel,
        (where, q, v, mid, far_got, near_got, gain, cot, lifted, stats),
        [VMEM] * 9,
        (arr((2, heads, WINDOW, GROUP), F32), arr((rows, feats), F32), arr((2, rows), F32), arr((2, 2 * SIDE, feats), BF16)),
        (VMEM,) * 4,
        [
            pltpu.VMEM((2, SIDE + BLOCK, GROUP), F32),
            pltpu.VMEM((2, heads, SIDE + BLOCK, GROUP), F32),
            pltpu.VMEM((2, 2 * heads, GROUP), F32),
        ],
        10**9,
    )
    sums = lax.all_gather(sums, "head")
    far_piece, near_piece, ds, dout = call(
        pieces_kernel,
        (where, q, v, mid, side, gain, cot, weights, attended, sums),
        [VMEM] * 9,
        (rim, rim, arr((2, heads, WINDOW, GROUP), BF16), whole),
        (VMEM,) * 4,
        [],
        10**9,
    )
    far_back = far_swap(far_piece)
    near_back = near_swap(near_piece)
    own, normed, query_grad = call(
        own_kernel,
        (where, q, k, mid, side, gain, weights, attended, sums, ds, dout),
        [VMEM] * 10,
        (arr((2, rows, feats), F32), whole, whole),
        (VMEM, HBM, HBM),
        [pltpu.VMEM((rows, feats), BF16), pltpu.VMEM((rows, feats), BF16), dma((3,))],
        10**9,
    )
    key_grad, value_grad = call(
        final_kernel,
        (where, own, far_back, near_back),
        [VMEM] * 3,
        (whole, whole),
        (HBM, HBM),
        [pltpu.VMEM((rows, feats), BF16), pltpu.VMEM((rows, feats), BF16), pltpu.VMEM((2, 2 * SIDE, feats), BF16), dma((4,))],
        10**8,
    )
    return normed, query_grad, key_grad, value_grad


def solution(mesh):
    in_specs = (P("seq", "head"), P("seq", "head"), P("seq", "head"), P("head"), P("seq", "head"))
    out_specs = (P("seq", "head"), P("seq", "head"), P("seq", "head"), P("seq", "head"))
    return jax.shard_map(local, mesh=mesh, in_specs=in_specs, out_specs=out_specs, check_vma=False)
```

```python
from functools import partial

import jax
import jax.numpy as jnp
from jax import lax
from jax.experimental import pallas as pl
from jax.experimental.pallas import tpu as pltpu
from jax.sharding import PartitionSpec as P

HEADS = 16
HDIM = 128
BLOCK = 16
SCALE = HDIM**-0.5
F32 = jnp.float32
BF16 = jnp.bfloat16

SIDE = 3 * BLOCK
RIM = SIDE + BLOCK
OWN_RAW = 9 * BLOCK
OWN_MID = 3 * BLOCK
OWN = OWN_RAW + OWN_MID
WINDOW = RIM + OWN
GROUP = 128


def dot(a, b, ca, cb):
    return lax.dot_general(a, b, (((ca,), (cb,)), ((), ())), preferred_element_type=F32)


def parity():
    return lax.axis_index("seq") % 2


def has_sides():
    index = lax.axis_index("seq")
    return (index > 0).astype(jnp.int32), (index < lax.axis_size("seq") - 1).astype(jnp.int32)


def pool_matrix(rows):
    shape = (rows // 4 + rows // 16, rows)
    out_row = lax.broadcasted_iota(jnp.int32, shape, 0)
    row = lax.broadcasted_iota(jnp.int32, shape, 1)
    middle = (row // 4 == out_row).astype(F32) * 0.5
    coarse = (row // 16 == out_row - rows // 4).astype(F32) * 0.25
    return jnp.where(out_row < rows // 4, middle, coarse).astype(BF16)


def pack_side(i, k_or_v, upper, mid_ref, coarse_ref, out_ref):
    raw_at = pl.multiple_of(upper * (k_or_v.shape[0] - BLOCK), BLOCK)
    mid_at = pl.multiple_of(upper * (mid_ref.shape[1] - BLOCK), BLOCK)
    base = i * SIDE
    out_ref[base : base + BLOCK] = k_or_v[pl.ds(raw_at, BLOCK)]
    out_ref[base + BLOCK : base + 2 * BLOCK] = mid_ref[i, pl.ds(mid_at, BLOCK)]
    out_ref[base + 2 * BLOCK : base + 3 * BLOCK] = coarse_ref[i]


def pack_kernel(k_hbm, v_hbm, k_ref, v_ref, far_ref, near_ref, mid_ref, coarse_ref, sems):
    copies = [pltpu.make_async_copy(k_hbm, k_ref, sems.at[0]), pltpu.make_async_copy(v_hbm, v_ref, sems.at[1])]
    for copy in copies:
        copy.start()
    rows = k_ref.shape[0]
    mids = rows // 4
    upper = parity()
    pool = pool_matrix(rows)
    for i, ref in enumerate((k_ref, v_ref)):
        copies[i].wait()
        pooled = dot(pool, ref[...], 1, 0).astype(BF16)
        mid_ref[i] = pooled[:mids]
        coarse_ref[i] = pooled[mids:]
        pack_side(i, ref, upper, mid_ref, coarse_ref, far_ref)
        pack_side(i, ref, 1 - upper, mid_ref, coarse_ref, near_ref)


def place_sides(odd, far_ref, near_ref, side_ref):
    @pl.when(odd == 0)
    def _():
        side_ref[0] = far_ref[...]
        side_ref[1] = near_ref[...]

    @pl.when(odd == 1)
    def _():
        side_ref[0] = near_ref[...]
        side_ref[1] = far_ref[...]


def own_rows(i, g, cols, raw_ref, mid_ref):
    raw_at, mid_at = (g * (raw_ref.shape[0] - OWN_RAW), g * (mid_ref.shape[1] - OWN_MID))
    return [raw_ref[raw_at : raw_at + OWN_RAW, cols], mid_ref[i, mid_at : mid_at + OWN_MID, cols]]


def side_rows(i, g, cols, side_ref):
    base = i * SIDE
    return [side_ref[g, base : base + SIDE, cols], side_ref[1 - g, base + 2 * BLOCK : base + SIDE, cols]]


def window(i, g, cols, side_ref, raw_ref, mid_ref):
    return jnp.concatenate([*side_rows(i, g, cols, side_ref), *own_rows(i, g, cols, raw_ref, mid_ref)], axis=0)


def allowed(g, has_below, has_above):
    shape = (WINDOW, GROUP)
    kb = lax.broadcasted_iota(jnp.int32, shape, 0) // BLOCK
    qb = lax.broadcasted_iota(jnp.int32, shape, 1) // BLOCK
    qm = qb // 4
    raw_gap = kb - 4 - g - qb
    mid_gap = kb - 13 - g - qm
    edge_raw = qb == (7 if g else 0)
    edge_mid = qm == (1 if g else 0)
    one = jnp.ones(shape, jnp.int32)
    none = jnp.zeros(shape, jnp.int32)
    own = jnp.where(kb < 13, jnp.where(jnp.abs(raw_gap) <= 1, one, none), jnp.where(jnp.abs(mid_gap) == 1, one, none))
    side = jnp.where(kb == 0, jnp.where(edge_raw, one, none), jnp.where(kb == 1, jnp.where(edge_mid, one, none), one))
    valid_side, valid_other = (has_above, has_below) if g else (has_below, has_above)
    return jnp.where(kb < 3, side * valid_side, jnp.where(kb == 3, one * valid_other, own))


def local_kernel(
    k_ref, v_ref, mid_ref, q_hbm, cot_hbm, gain_hbm,
    q_ref, gain_ref, scaled_ref, lifted_ref, stats_ref, mix_ref, bias_ref, cot_ref, own_bias, sems,
):
    copies = [
        pltpu.make_async_copy(src, dst, sems.at[n])
        for n, (src, dst) in enumerate([(q_hbm, q_ref), (cot_hbm, cot_ref), (gain_hbm, gain_ref)])
    ]
    for copy in copies:
        copy.start()
    for g in range(2):
        bias = jnp.where(allowed(g, *has_sides()) == 1, 0.0, -1e30)
        bias_ref[g] = bias[:RIM]
        own_bias[g] = bias[RIM:]
    for copy in copies:
        copy.wait()
    heads = lifted_ref.shape[1]
    for g in range(2):
        rows = slice(g * GROUP, (g + 1) * GROUP)
        for h in range(heads):
            cols = slice(h * HDIM, (h + 1) * HDIM)
            keys = jnp.concatenate(own_rows(0, g, cols, k_ref, mid_ref), axis=0)
            scores = dot(keys, q_ref[rows, cols], 1, 1) * SCALE + own_bias[g]
            highest = jnp.max(scores, axis=0, keepdims=True)
            lifted = jnp.exp(scores - highest)
            lifted_ref[g, h] = lifted
            stats_ref[g, h : h + 1] = highest
            stats_ref[g, heads + h : heads + h + 1] = jnp.sum(lifted, axis=0, keepdims=True)
            scaled_ref[g, h] = (cot_ref[rows, cols].astype(F32) * gain_ref[:, cols]).T
    for g in range(2):
        for h in range(heads):
            values = jnp.concatenate(own_rows(1, g, slice(h * HDIM, (h + 1) * HDIM), v_ref, mid_ref), axis=0)
            mix_ref[g, h] = dot(values, lifted_ref[g, h].astype(BF16), 0, 0)


def forward_kernel(
    q_ref, far_ref, near_ref, bias_ref, scaled_ref, stats_ref, mix_ref,
    side_ref, side_w, own_scale, att_ref, sums_ref, side_stats,
):
    place_sides(parity(), far_ref, near_ref, side_ref)
    heads = mix_ref.shape[1]
    for g in range(2):
        rows = slice(g * GROUP, (g + 1) * GROUP)
        for h in range(heads):
            cols = slice(h * HDIM, (h + 1) * HDIM)
            keys = jnp.concatenate(side_rows(0, g, cols, side_ref), axis=0)
            scores = dot(keys, q_ref[rows, cols], 1, 1) * SCALE + bias_ref[g]
            highest = jnp.max(scores, axis=0, keepdims=True)
            lifted = jnp.exp(scores - highest)
            side_w[g, h] = lifted
            side_stats[g, h : h + 1] = highest
            side_stats[g, heads + h : heads + h + 1] = jnp.sum(lifted, axis=0, keepdims=True)
    for g in range(2):
        rows = slice(g * GROUP, (g + 1) * GROUP)
        own_high, side_high = stats_ref[g, :heads], side_stats[g, :heads]
        highest = jnp.maximum(own_high, side_high)
        own_part, side_part = jnp.exp(own_high - highest), jnp.exp(side_high - highest)
        inverse = 1.0 / (stats_ref[g, heads:] * own_part + side_stats[g, heads:] * side_part)
        own_part, side_part = own_part * inverse, side_part * inverse
        own_scale[g] = own_part
        squares = jnp.zeros((HDIM, GROUP), F32)
        crossed = jnp.zeros((HDIM, GROUP), F32)
        for h in range(heads):
            cols = slice(h * HDIM, (h + 1) * HDIM)
            weights = side_w[g, h] * side_part[h : h + 1]
            side_w[g, h] = weights
            values = jnp.concatenate(side_rows(1, g, cols, side_ref), axis=0)
            mixed = mix_ref[g, h] * own_part[h : h + 1] + dot(values, weights.astype(BF16), 0, 0)
            att_ref[g, h] = mixed
            squares += mixed * mixed
            crossed += mixed * scaled_ref[g, h]
        sums_ref[0:1, rows] = jnp.sum(squares, axis=0, keepdims=True)
        sums_ref[1:2, rows] = jnp.sum(crossed, axis=0, keepdims=True)


def row_factors(sums_ref):
    feat_all = HEADS * HDIM
    totals = sums_ref[0] + sums_ref[1]
    factor = lax.rsqrt(totals[0:1] / feat_all + 1e-06)
    return factor, factor * factor * factor * totals[1:2] / feat_all


def side_piece(g, q_ref, side_w, ds_ref, dout_ref, out_ref):
    half = q_ref.shape[0] // 2
    mine = pl.ds(pl.multiple_of(g * half, half), half)
    other = pl.ds(pl.multiple_of((1 - g) * half, half), half)
    blank = jnp.zeros((2 * BLOCK, GROUP), BF16)
    for h in range(side_w.shape[1]):
        cols = slice(h * HDIM, (h + 1) * HDIM)
        lefts = [
            jnp.concatenate(
                [ref[g, h, :SIDE].astype(BF16), jnp.concatenate([blank, ref[1 - g, h, SIDE:RIM].astype(BF16)], axis=0)], axis=1
            )
            for ref in (ds_ref, side_w)
        ]
        queries = jnp.concatenate([q_ref[mine, cols], q_ref[other, cols]], axis=0)
        out_ref[:SIDE, cols] = dot(lefts[0], queries, 1, 0).astype(BF16)
        douts = jnp.concatenate([dout_ref[g, h], dout_ref[1 - g, h]], axis=1)
        out_ref[SIDE:, cols] = dot(lefts[1], douts, 1, 1).astype(BF16)


def pieces_kernel(
    q_ref, v_ref, mid_ref, side_ref, scaled_ref, lifted_ref, side_w, own_scale, att_ref, sums_ref,
    far_out, near_out, ds_ref, dout_ref,
):
    factor, cross = row_factors(sums_ref)
    for h in range(side_w.shape[1]):
        cols = slice(h * HDIM, (h + 1) * HDIM)
        for g in range(2):
            rows = slice(g * GROUP, (g + 1) * GROUP)
            grad_out = (factor[:, rows] * scaled_ref[g, h] - cross[:, rows] * att_ref[g, h]).astype(BF16)
            dout_ref[g, h] = grad_out
            grad_w = dot(window(1, g, cols, side_ref, v_ref, mid_ref), grad_out, 1, 0)
            weights = jnp.concatenate([side_w[g, h], lifted_ref[g, h] * own_scale[g, h : h + 1]], axis=0)
            middle = jnp.sum(weights * grad_w, axis=0, keepdims=True)
            ds_ref[g, h] = (weights * (grad_w - middle) * SCALE).astype(BF16)
    upper = parity()
    side_piece(upper, q_ref, side_w, ds_ref, dout_ref, far_out)
    side_piece(1 - upper, q_ref, side_w, ds_ref, dout_ref, near_out)


def spread_matrix(rows, kinds):
    parts = []
    for first, factor, weight, count in kinds:
        row = lax.broadcasted_iota(jnp.int32, (rows, count), 0)
        at = lax.broadcasted_iota(jnp.int32, (rows, count), 1)
        parts.append((((row - first) // factor == at) & (row >= first)).astype(F32) * weight)
    return jnp.concatenate(parts, axis=1).astype(BF16)


def own_kernel(
    q_ref, k_ref, mid_ref, side_ref, gain_ref, lifted_ref, own_scale, att_ref, sums_ref, ds_ref, dout_ref,
    own_ref, spread_ref, normed_hbm, dq_hbm, normed_ref, dq_ref, mid_grad, sems,
):
    rows_all = q_ref.shape[0]
    heads = lifted_ref.shape[1]
    factor, _ = row_factors(sums_ref)
    copies = []
    spread = spread_matrix(rows_all, [(0, 4, 0.5, rows_all // 4)])
    for h in range(heads):
        cols = slice(h * HDIM, (h + 1) * HDIM)
        inner = []
        for g in range(2):
            rows = slice(g * GROUP, (g + 1) * GROUP)
            normed_ref[rows, cols] = ((att_ref[g, h] * factor[:, rows]).T * gain_ref[:, cols]).astype(BF16)
            ds = ds_ref[g, h]
            keys = window(0, g, cols, side_ref, k_ref, mid_ref)
            dq_ref[rows, cols] = dot(ds, keys, 0, 0).astype(BF16)
            low = (lifted_ref[g, h] * own_scale[g, h : h + 1]).astype(BF16)
            inner.append((dot(ds[RIM:], q_ref[rows, cols], 1, 0), dot(low, dout_ref[g, h], 1, 1)))
        if h % (heads // 2) == heads // 2 - 1:
            done = pl.ds((h + 1 - heads // 2) * HDIM, heads // 2 * HDIM)
            for ref, hbm in ((normed_ref, normed_hbm), (dq_ref, dq_hbm)):
                copies.append(pltpu.make_async_copy(ref.at[:, done], hbm.at[:, done], sems.at[len(copies)]))
                copies[-1].start()
        for i in range(2):
            lower, upper = inner[0][i], inner[1][i]
            both_raw = 2 * OWN_RAW - rows_all
            raw = jnp.concatenate(
                [lower[: OWN_RAW - both_raw], lower[OWN_RAW - both_raw : OWN_RAW] + upper[:both_raw], upper[both_raw:OWN_RAW]],
                axis=0,
            )
            own_ref[i, :, cols] = raw
            low_mid, up_mid = lower[OWN_RAW:], upper[OWN_RAW:]
            both_mid = 2 * OWN_MID - rows_all // 4
            mid_grad[i, :, cols] = jnp.concatenate(
                [low_mid[: OWN_MID - both_mid], low_mid[OWN_MID - both_mid :] + up_mid[:both_mid], up_mid[both_mid:]], axis=0
            ).astype(BF16)
    for i in range(2):
        own_ref[i] += dot(spread, mid_grad[i], 1, 0)
    for g in range(2):
        raw_at, mid_at = (rows_all - BLOCK, rows_all - 4 * BLOCK) if g else (0, 0)
        spread_ref[g] = spread_matrix(rows_all, [(raw_at, 1, 1.0, BLOCK), (mid_at, 4, 0.5, BLOCK), (0, 16, 0.25, BLOCK)])
    for copy in copies:
        copy.wait()


def final_kernel(own_ref, spread_ref, far_ref, near_ref, dk_hbm, dv_hbm, dk_ref, dv_ref, sems):
    rows = own_ref.shape[1]
    upper = parity()
    both = jnp.concatenate([spread_ref[upper], spread_ref[1 - upper]], axis=1)
    copies = []
    for i, (out_ref, hbm) in enumerate(((dk_ref, dk_hbm), (dv_ref, dv_hbm))):
        got = jnp.concatenate([far_ref[i * SIDE : (i + 1) * SIDE], near_ref[i * SIDE : (i + 1) * SIDE]], axis=0)
        for part in range(2):
            at = slice(part * (rows // 2), (part + 1) * (rows // 2))
            out_ref[at] = (own_ref[i, at] + dot(both[at], got, 1, 0)).astype(BF16)
            copies.append(pltpu.make_async_copy(out_ref.at[at], hbm.at[at], sems.at[len(copies)]))
            copies[-1].start()
    for copy in copies:
        copy.wait()


VMEM = pl.BlockSpec(memory_space=pltpu.VMEM)
HBM = pl.BlockSpec(memory_space=pltpu.HBM)


def call(kernel, args, outs, scratch, flops):
    placed = [pltpu.with_memory_space_constraint(x, pltpu.HBM) if space is HBM else x for x, space in args]
    return pl.pallas_call(
        kernel,
        out_shape=tuple(shape for shape, _ in outs),
        in_specs=[space for _, space in args],
        out_specs=tuple(space for _, space in outs),
        scratch_shapes=scratch,
        compiler_params=pltpu.CompilerParams(vmem_limit_bytes=24 * 2**20),
        cost_estimate=pl.CostEstimate(flops=flops, bytes_accessed=4 * 2**20, transcendentals=0),
    )(*placed)


def on(space, *xs):
    return [(x, space) for x in xs]


def far_swap(x):
    pairs = [(i, i + 1) for i in range(1, lax.axis_size("seq") - 1, 2)]
    return lax.ppermute(x, "seq", pairs + [(j, i) for i, j in pairs])


def near_swap(x):
    pairs = [(i, i + 1) for i in range(0, lax.axis_size("seq"), 2)]
    return lax.ppermute(x, "seq", pairs + [(j, i) for i, j in pairs])


def local(queries, key_vectors, value_vectors, norm_gain, cotangent):
    rows, feats = queries.shape
    heads = feats // HDIM
    gain = norm_gain.reshape(1, feats)
    arr = jax.ShapeDtypeStruct
    dma = pltpu.SemaphoreType.DMA
    whole = arr((rows, feats), BF16)
    rim = arr((2 * SIDE, feats), BF16)
    tiles = arr((2, heads, HDIM, GROUP), F32)
    k, v, far, near, mid = call(
        pack_kernel,
        on(HBM, key_vectors, value_vectors),
        on(VMEM, whole, whole, rim, rim, arr((2, rows // 4, feats), BF16)),
        [pltpu.VMEM((2, BLOCK, feats), BF16), dma((2,))],
        10**8,
    )
    far_got = far_swap(far)
    near_got = near_swap(near)
    q, gain, scaled, lifted, stats, mix, bias = call(
        local_kernel,
        on(VMEM, k, v, mid) + on(HBM, queries, cotangent, gain),
        on(
            VMEM, whole, arr((1, feats), F32), tiles, arr((2, heads, OWN, GROUP), F32), arr((2, 2 * heads, GROUP), F32),
            tiles, arr((2, RIM, GROUP), F32),
        ),
        [pltpu.VMEM((rows, feats), BF16), pltpu.VMEM((2, OWN, GROUP), F32), dma((3,))],
        10**9,
    )
    side, side_w, own_scale, attended, sums = call(
        forward_kernel,
        on(VMEM, q, far_got, near_got, bias, scaled, stats, mix),
        on(
            VMEM, arr((2, 2 * SIDE, feats), BF16), arr((2, heads, RIM, GROUP), F32), arr((2, heads, GROUP), F32),
            tiles, arr((2, rows), F32),
        ),
        [pltpu.VMEM((2, 2 * heads, GROUP), F32)],
        10**9,
    )
    sums = lax.all_gather(sums, "head")
    far_piece, near_piece, ds, dout = call(
        pieces_kernel,
        on(VMEM, q, v, mid, side, scaled, lifted, side_w, own_scale, attended, sums),
        on(VMEM, rim, rim, arr((2, heads, WINDOW, GROUP), BF16), arr((2, heads, HDIM, GROUP), BF16)),
        [],
        10**9,
    )
    far_back = far_swap(far_piece)
    near_back = near_swap(near_piece)
    own, spread, normed, query_grad = call(
        own_kernel,
        on(VMEM, q, k, mid, side, gain, lifted, own_scale, attended, sums, ds, dout),
        on(VMEM, arr((2, rows, feats), F32), arr((2, rows, SIDE), BF16)) + on(HBM, whole, whole),
        [pltpu.VMEM((rows, feats), BF16), pltpu.VMEM((rows, feats), BF16), pltpu.VMEM((2, rows // 4, feats), BF16), dma((4,))],
        10**9,
    )
    key_grad, value_grad = call(
        final_kernel,
        on(VMEM, own, spread, far_back, near_back),
        on(HBM, whole, whole),
        [pltpu.VMEM((rows, feats), BF16), pltpu.VMEM((rows, feats), BF16), dma((4,))],
        10**8,
    )
    return normed, query_grad, key_grad, value_grad


def solution(mesh):
    in_specs = (P("seq", "head"), P("seq", "head"), P("seq", "head"), P("head"), P("seq", "head"))
    out_specs = (P("seq", "head"), P("seq", "head"), P("seq", "head"), P("seq", "head"))
    return jax.shard_map(local, mesh=mesh, in_specs=in_specs, out_specs=out_specs, check_vma=False)
```

```python
import jax
import jax.numpy as jnp
from jax import lax
from jax.experimental import pallas as pl
from jax.experimental.pallas import tpu as pltpu
from jax.sharding import PartitionSpec as P

HEADS = 16
HDIM = 128
BLOCK = 16
SCALE = HDIM**-0.5
F32 = jnp.float32
BF16 = jnp.bfloat16

SIDE = 3 * BLOCK
RIM = SIDE + BLOCK
KEPT = BLOCK - 4
PACKED = BLOCK + 2 * KEPT
OWN_RAW = 9 * BLOCK
OWN_MID = 3 * BLOCK
OWN = OWN_RAW + OWN_MID
WINDOW = RIM + OWN
GROUP = 128


def dot(a, b, ca, cb):
    return lax.dot_general(a, b, (((ca,), (cb,)), ((), ())), preferred_element_type=F32)


def parity():
    return lax.axis_index("seq") % 2


def has_sides():
    index = lax.axis_index("seq")
    return (index > 0).astype(jnp.int32), (index < lax.axis_size("seq") - 1).astype(jnp.int32)


def iotas(shape):
    return lax.broadcasted_iota(jnp.int32, shape, 0), lax.broadcasted_iota(jnp.int32, shape, 1)


def one_if(flag, weight=1.0):
    return jnp.where(flag, weight, 0.0)


def pack_entries(p, row, rows, upper):
    middle = (1 - upper) * 4 + upper * (rows // 4 - BLOCK) - BLOCK
    coarse = (1 - upper) * 4 - BLOCK - KEPT
    raw_hit = one_if(p + upper * (rows - BLOCK) == row)
    mid_hit = one_if(p + middle == row // 4, 0.5)
    coarse_hit = one_if(p + coarse == row // 16, 0.25)
    return jnp.where(p < BLOCK, raw_hit, jnp.where(p < BLOCK + KEPT, mid_hit, coarse_hit))


def edge_entries(o, row, rows, upper):
    raw_hit = one_if(o + upper * (rows - BLOCK) == row)
    mid_hit = one_if(o - BLOCK + upper * (rows // 4 - BLOCK) == row // 4, 0.5)
    return jnp.where(o < BLOCK, raw_hit, jnp.where(o < 2 * BLOCK, mid_hit, one_if(o - 2 * BLOCK == row // 16, 0.25)))


def unpack_entries(o, n, upper):
    j, c = o - BLOCK, o - 2 * BLOCK
    from_raw = one_if((n < BLOCK) & (n // 4 == j - 12 * upper), 0.5)
    mid_hit = from_raw + one_if((n >= BLOCK) & (n < BLOCK + KEPT) & (n - BLOCK == j - 4 * (1 - upper)))
    coarse_hit = (
        one_if((n < BLOCK) & (c == 15 * upper), 0.25)
        + one_if((n >= BLOCK) & (n < BLOCK + KEPT) & ((n - BLOCK) // 4 == c - 1 - 11 * upper), 0.5)
        + one_if((n >= BLOCK + KEPT) & (n - BLOCK - KEPT == c - 4 * (1 - upper)))
    )
    return jnp.where(o < BLOCK, one_if(o == n), jnp.where(o < 2 * BLOCK, mid_hit, coarse_hit))


def unpack_both(o, n, upper):
    same = ((o >= SIDE) & (n >= PACKED)) | ((o < SIDE) & (n < PACKED))
    return jnp.where(same, unpack_entries(jnp.where(o >= SIDE, o - SIDE, o), jnp.where(n >= PACKED, n - PACKED, n), upper), 0.0)


def pack_kernel(k_hbm, v_hbm, k_ref, v_ref, far_ref, near_ref, mid_ref, sems):
    copies = [pltpu.make_async_copy(k_hbm, k_ref, sems.at[0]), pltpu.make_async_copy(v_hbm, v_ref, sems.at[1])]
    for copy in copies:
        copy.start()
    rows = k_ref.shape[0]
    mids = rows // 4
    upper = parity()
    out_row, row = iotas((mids, rows))
    parts = [one_if(out_row == row // 4, 0.5)]
    p, row = iotas((PACKED, rows))
    parts += [pack_entries(p, row, rows, edge) for edge in (upper, 1 - upper)]
    pool = jnp.concatenate(parts, axis=0).astype(BF16)
    pooled = []
    for i, ref in enumerate((k_ref, v_ref)):
        copies[i].wait()
        pooled.append(dot(pool, ref[...], 1, 0))
    for at, out_ref in ((mids, far_ref), (mids + PACKED, near_ref)):
        out_ref[...] = jnp.concatenate([x[at : at + PACKED] for x in pooled], axis=0).astype(BF16)
    for i in range(2):
        mid_ref[i] = pooled[i][:mids].astype(BF16)


def own_rows(i, g, cols, raw_ref, mid_ref):
    raw_at, mid_at = (g * (raw_ref.shape[0] - OWN_RAW), g * (mid_ref.shape[1] - OWN_MID))
    return [raw_ref[raw_at : raw_at + OWN_RAW, cols], mid_ref[i, mid_at : mid_at + OWN_MID, cols]]


def side_rows(i, g, cols, side_ref):
    base = i * SIDE
    return [side_ref[g, base : base + SIDE, cols], side_ref[1 - g, base + 2 * BLOCK : base + SIDE, cols]]


def window(i, g, cols, side_ref, raw_ref, mid_ref):
    return jnp.concatenate([*side_rows(i, g, cols, side_ref), *own_rows(i, g, cols, raw_ref, mid_ref)], axis=0)


def allowed(g, has_below, has_above):
    shape = (WINDOW, GROUP)
    kb = lax.broadcasted_iota(jnp.int32, shape, 0) // BLOCK
    qb = lax.broadcasted_iota(jnp.int32, shape, 1) // BLOCK
    qm = qb // 4
    raw_gap = kb - 4 - g - qb
    mid_gap = kb - 13 - g - qm
    edge_raw = qb == (7 if g else 0)
    edge_mid = qm == (1 if g else 0)
    one = jnp.ones(shape, jnp.int32)
    none = jnp.zeros(shape, jnp.int32)
    own = jnp.where(kb < 13, jnp.where(jnp.abs(raw_gap) <= 1, one, none), jnp.where(jnp.abs(mid_gap) == 1, one, none))
    side = jnp.where(kb == 0, jnp.where(edge_raw, one, none), jnp.where(kb == 1, jnp.where(edge_mid, one, none), one))
    valid_side, valid_other = (has_above, has_below) if g else (has_below, has_above)
    return jnp.where(kb < 3, side * valid_side, jnp.where(kb == 3, one * valid_other, own))


def local_kernel(
    k_ref, v_ref, mid_ref, q_hbm, cot_hbm, gain_hbm,
    q_ref, gain_ref, scaled_ref, lifted_ref, stats_ref, mix_ref, bias_ref, unfold_ref, fold_ref, cot_ref, own_bias, sems,
):
    copies = [
        pltpu.make_async_copy(src, dst, sems.at[n])
        for n, (src, dst) in enumerate([(q_hbm, q_ref), (cot_hbm, cot_ref), (gain_hbm, gain_ref)])
    ]
    for copy in copies:
        copy.start()
    for g in range(2):
        bias = jnp.where(allowed(g, *has_sides()) == 1, 0.0, -1e30)
        bias_ref[g] = bias[:RIM]
        own_bias[g] = bias[RIM:]
        unfold_ref[g] = unpack_both(*iotas((2 * SIDE, 2 * PACKED)), 1 - g).astype(BF16)
        fold_ref[g] = unpack_both(*iotas((2 * PACKED, 2 * SIDE))[::-1], 1 - g).astype(BF16)
    for copy in copies:
        copy.wait()
    heads = lifted_ref.shape[1]
    for g in range(2):
        rows = slice(g * GROUP, (g + 1) * GROUP)
        for h in range(heads):
            cols = slice(h * HDIM, (h + 1) * HDIM)
            keys = jnp.concatenate(own_rows(0, g, cols, k_ref, mid_ref), axis=0)
            scores = dot(keys, q_ref[rows, cols], 1, 1) * SCALE + own_bias[g]
            highest = jnp.max(scores, axis=0, keepdims=True)
            lifted = jnp.exp(scores - highest).astype(BF16)
            lifted_ref[g, h] = lifted
            stats_ref[g, h : h + 1] = highest
            stats_ref[g, heads + h : heads + h + 1] = jnp.sum(lifted.astype(F32), axis=0, keepdims=True)
            scaled_ref[g, h] = (cot_ref[rows, cols].astype(F32) * gain_ref[:, cols]).T
    for g in range(2):
        for h in range(heads):
            values = jnp.concatenate(own_rows(1, g, slice(h * HDIM, (h + 1) * HDIM), v_ref, mid_ref), axis=0)
            mix_ref[g, h] = dot(values, lifted_ref[g, h], 0, 0)


def forward_kernel(
    q_ref, far_ref, near_ref, bias_ref, unfold_ref, scaled_ref, stats_ref, mix_ref,
    side_ref, side_lifted, own_scale, side_scale, att_ref, sums_ref, side_stats,
):
    odd = parity()
    side_ref[odd] = dot(unfold_ref[odd], far_ref[...], 1, 0).astype(BF16)
    side_ref[1 - odd] = dot(unfold_ref[1 - odd], near_ref[...], 1, 0).astype(BF16)
    heads = mix_ref.shape[1]
    for g in range(2):
        rows = slice(g * GROUP, (g + 1) * GROUP)
        for h in range(heads):
            cols = slice(h * HDIM, (h + 1) * HDIM)
            keys = jnp.concatenate(side_rows(0, g, cols, side_ref), axis=0)
            scores = dot(keys, q_ref[rows, cols], 1, 1) * SCALE + bias_ref[g]
            highest = jnp.max(scores, axis=0, keepdims=True)
            lifted = jnp.exp(scores - highest).astype(BF16)
            side_lifted[g, h] = lifted
            side_stats[g, h : h + 1] = highest
            side_stats[g, heads + h : heads + h + 1] = jnp.sum(lifted.astype(F32), axis=0, keepdims=True)
    for g in range(2):
        rows = slice(g * GROUP, (g + 1) * GROUP)
        own_high, side_high = stats_ref[g, :heads], side_stats[g, :heads]
        highest = jnp.maximum(own_high, side_high)
        own_part, side_part = jnp.exp(own_high - highest), jnp.exp(side_high - highest)
        inverse = 1.0 / (stats_ref[g, heads:] * own_part + side_stats[g, heads:] * side_part)
        own_part, side_part = own_part * inverse, side_part * inverse
        own_scale[g] = own_part
        side_scale[g] = side_part
        squares = jnp.zeros((HDIM, GROUP), F32)
        crossed = jnp.zeros((HDIM, GROUP), F32)
        for h in range(heads):
            cols = slice(h * HDIM, (h + 1) * HDIM)
            values = jnp.concatenate(side_rows(1, g, cols, side_ref), axis=0)
            mixed = mix_ref[g, h] * own_part[h : h + 1] + dot(values, side_lifted[g, h], 0, 0) * side_part[h : h + 1]
            att_ref[g, h] = mixed
            squares += mixed * mixed
            crossed += mixed * scaled_ref[g, h]
        sums_ref[0:1, rows] = jnp.sum(squares, axis=0, keepdims=True)
        sums_ref[1:2, rows] = jnp.sum(crossed, axis=0, keepdims=True)


def row_factors(sums_ref):
    feat_all = HEADS * HDIM
    totals = sums_ref[0] + sums_ref[1]
    factor = lax.rsqrt(totals[0:1] / feat_all + 1e-06)
    return factor, factor * factor * factor * totals[1:2] / feat_all


def side_piece(g, q_ref, side_w, ds_ref, dout_ref, out_ref):
    half = q_ref.shape[0] // 2
    mine = pl.ds(pl.multiple_of(g * half, half), half)
    other = pl.ds(pl.multiple_of((1 - g) * half, half), half)
    blank = jnp.zeros((2 * BLOCK, GROUP), BF16)
    for h in range(side_w.shape[1]):
        cols = slice(h * HDIM, (h + 1) * HDIM)
        lefts = [
            jnp.concatenate([ref[g, h, :SIDE], jnp.concatenate([blank, ref[1 - g, h, SIDE:RIM]], axis=0)], axis=1)
            for ref in (ds_ref, side_w)
        ]
        queries = jnp.concatenate([q_ref[mine, cols], q_ref[other, cols]], axis=0)
        out_ref[:SIDE, cols] = dot(lefts[0], queries, 1, 0).astype(BF16)
        douts = jnp.concatenate([dout_ref[g, h], dout_ref[1 - g, h]], axis=1)
        out_ref[SIDE:, cols] = dot(lefts[1], douts, 1, 1).astype(BF16)


def pieces_kernel(
    q_ref, side_ref, scaled_ref, side_lifted, side_scale, att_ref, sums_ref,
    far_out, ds_ref, side_w, dout_ref, delta_ref,
):
    factor, cross = row_factors(sums_ref)
    heads = side_w.shape[1]
    for h in range(heads):
        cols = slice(h * HDIM, (h + 1) * HDIM)
        for g in range(2):
            rows = slice(g * GROUP, (g + 1) * GROUP)
            attended = att_ref[g, h]
            grad_out = (factor[:, rows] * scaled_ref[g, h] - cross[:, rows] * attended).astype(BF16)
            dout_ref[g, h] = grad_out
            delta = jnp.sum(grad_out.astype(F32) * attended, axis=0, keepdims=True)
            delta_ref[g, h : h + 1] = delta
            values = jnp.concatenate(side_rows(1, g, cols, side_ref), axis=0)
            weights = side_lifted[g, h].astype(F32) * side_scale[g, h : h + 1]
            side_w[g, h] = weights.astype(BF16)
            ds_ref[g, h] = (weights * (dot(values, grad_out, 1, 0) - delta) * SCALE).astype(BF16)
    side_piece(parity(), q_ref, side_w, ds_ref, dout_ref, far_out)


def near_kernel(q_ref, side_w, ds_ref, dout_ref, fold_ref, near_out, piece_ref):
    side = 1 - parity()
    side_piece(side, q_ref, side_w, ds_ref, dout_ref, piece_ref)
    near_out[...] = dot(fold_ref[side], piece_ref[...], 1, 0).astype(BF16)


def own_kernel(
    q_ref, k_ref, v_ref, mid_ref, side_ref, gain_ref, lifted_ref, own_scale, att_ref, sums_ref, ds_ref, dout_ref, delta_ref,
    own_ref, mid_grad, spread_ref, normed_hbm, dq_hbm, normed_ref, dq_ref, own_w, own_ds, sems,
):
    odd = parity()
    rows_all = q_ref.shape[0]
    heads = lifted_ref.shape[1]
    for h in range(heads):
        cols = slice(h * HDIM, (h + 1) * HDIM)
        for g in range(2):
            values = jnp.concatenate(own_rows(1, g, cols, v_ref, mid_ref), axis=0)
            weights = lifted_ref[g, h].astype(F32) * own_scale[g, h : h + 1]
            own_w[g, h] = weights.astype(BF16)
            own_ds[g, h] = (weights * (dot(values, dout_ref[g, h], 1, 0) - delta_ref[g, h : h + 1]) * SCALE).astype(BF16)
    factor, _ = row_factors(sums_ref)
    copies = []
    half = heads // 2
    for h in range(heads):
        cols = slice(h * HDIM, (h + 1) * HDIM)
        for g in range(2):
            rows = slice(g * GROUP, (g + 1) * GROUP)
            normed_ref[rows, cols] = ((att_ref[g, h] * factor[:, rows]).T * gain_ref[:, cols]).astype(BF16)
            keys = window(0, g, cols, side_ref, k_ref, mid_ref)
            dq_ref[rows, cols] = dot(jnp.concatenate([ds_ref[g, h], own_ds[g, h]], axis=0), keys, 0, 0).astype(BF16)
        if h % half == half - 1:
            done = pl.ds((h + 1 - half) * HDIM, half * HDIM)
            for ref, hbm in ((normed_ref, normed_hbm), (dq_ref, dq_hbm)):
                copies.append(pltpu.make_async_copy(ref.at[:, done], hbm.at[:, done], sems.at[len(copies)]))
                copies[-1].start()
    both_raw = 2 * OWN_RAW - rows_all
    both_mid = 2 * OWN_MID - rows_all // 4
    for h in range(heads):
        cols = slice(h * HDIM, (h + 1) * HDIM)
        inner = []
        for g in range(2):
            rows = slice(g * GROUP, (g + 1) * GROUP)
            inner.append((dot(own_ds[g, h], q_ref[rows, cols], 1, 0), dot(own_w[g, h], dout_ref[g, h], 1, 1)))
        for i in range(2):
            lower, upper = inner[0][i], inner[1][i]
            own_ref[i, :, cols] = jnp.concatenate(
                [lower[: OWN_RAW - both_raw], lower[OWN_RAW - both_raw : OWN_RAW] + upper[:both_raw], upper[both_raw:OWN_RAW]],
                axis=0,
            )
            low_mid, up_mid = lower[OWN_RAW:], upper[OWN_RAW:]
            mid_grad[i, :, cols] = jnp.concatenate(
                [low_mid[: OWN_MID - both_mid], low_mid[OWN_MID - both_mid :] + up_mid[:both_mid], up_mid[both_mid:]], axis=0
            ).astype(BF16)
    row, p = iotas((rows_all, PACKED))
    near_part = pack_entries(p, row, rows_all, 1 - odd)
    row, o = iotas((rows_all, SIDE))
    far_part = edge_entries(o, row, rows_all, odd)
    no_near, no_far = jnp.zeros((rows_all, PACKED), F32), jnp.zeros((rows_all, SIDE), F32)
    row, at = iotas((rows_all, rows_all // 4))
    mid_part = one_if(row // 4 == at, 0.5)
    spread_ref[0] = jnp.concatenate([far_part, no_far, near_part, no_near, mid_part], axis=1).astype(BF16)
    spread_ref[1] = jnp.concatenate([no_far, far_part, no_near, near_part, mid_part], axis=1).astype(BF16)
    for copy in copies:
        copy.wait()


def final_kernel(own_ref, mid_grad, spread_ref, far_ref, near_ref, dk_hbm, dv_hbm, dk_ref, dv_ref, sems):
    rows = own_ref.shape[1]
    copies = []
    for i, (out_ref, hbm) in enumerate(((dk_ref, dk_hbm), (dv_ref, dv_hbm))):
        got = jnp.concatenate([far_ref[...], near_ref[...], mid_grad[i]], axis=0)
        for part in range(2):
            at = slice(part * (rows // 2), (part + 1) * (rows // 2))
            out_ref[at] = (own_ref[i, at] + dot(spread_ref[i, at], got, 1, 0)).astype(BF16)
            copies.append(pltpu.make_async_copy(out_ref.at[at], hbm.at[at], sems.at[len(copies)]))
            copies[-1].start()
    for copy in copies:
        copy.wait()


VMEM = pl.BlockSpec(memory_space=pltpu.VMEM)
HBM = pl.BlockSpec(memory_space=pltpu.HBM)


def call(kernel, args, outs, scratch, flops):
    placed = [pltpu.with_memory_space_constraint(x, pltpu.HBM) if space is HBM else x for x, space in args]
    return pl.pallas_call(
        kernel,
        out_shape=tuple(shape for shape, _ in outs),
        in_specs=[space for _, space in args],
        out_specs=tuple(space for _, space in outs),
        scratch_shapes=scratch,
        compiler_params=pltpu.CompilerParams(vmem_limit_bytes=24 * 2**20),
        cost_estimate=pl.CostEstimate(flops=flops, bytes_accessed=flops // 256, transcendentals=0),
    )(*placed)


def on(space, *xs):
    return [(x, space) for x in xs]


def far_swap(x):
    pairs = [(i, i + 1) for i in range(1, lax.axis_size("seq") - 1, 2)]
    return lax.ppermute(x, "seq", pairs + [(j, i) for i, j in pairs])


def near_swap(x):
    pairs = [(i, i + 1) for i in range(0, lax.axis_size("seq"), 2)]
    return lax.ppermute(x, "seq", pairs + [(j, i) for i, j in pairs])


def local(queries, key_vectors, value_vectors, norm_gain, cotangent):
    rows, feats = queries.shape
    heads = feats // HDIM
    gain = norm_gain.reshape(1, feats)
    arr = jax.ShapeDtypeStruct
    dma = pltpu.SemaphoreType.DMA
    whole = arr((rows, feats), BF16)
    packed = arr((2 * PACKED, feats), BF16)
    mids = arr((2, rows // 4, feats), BF16)
    sides = pltpu.VMEM((2 * SIDE, feats), BF16)
    tiles = arr((2, heads, HDIM, GROUP), F32)
    k, v, far, near, mid = call(
        pack_kernel,
        on(HBM, key_vectors, value_vectors),
        on(VMEM, whole, whole, packed, packed, mids),
        [dma((2,))],
        10**8,
    )
    far_got = far_swap(far)
    near_got = near_swap(near)
    q, gain, scaled, lifted, stats, mix, bias, unfold, fold = call(
        local_kernel,
        on(VMEM, k, v, mid) + on(HBM, queries, cotangent, gain),
        on(
            VMEM, whole, arr((1, feats), F32), tiles, arr((2, heads, OWN, GROUP), BF16), arr((2, 2 * heads, GROUP), F32),
            tiles, arr((2, RIM, GROUP), F32), arr((2, 2 * SIDE, 2 * PACKED), BF16), arr((2, 2 * PACKED, 2 * SIDE), BF16),
        ),
        [pltpu.VMEM((rows, feats), BF16), pltpu.VMEM((2, OWN, GROUP), F32), dma((3,))],
        10**9,
    )
    scales = arr((2, heads, GROUP), F32)
    side_tiles = arr((2, heads, RIM, GROUP), BF16)
    rim = arr((2 * SIDE, feats), BF16)
    side, side_lifted, own_scale, side_scale, attended, sums = call(
        forward_kernel,
        on(VMEM, q, far_got, near_got, bias, unfold, scaled, stats, mix),
        on(VMEM, arr((2, 2 * SIDE, feats), BF16), side_tiles, scales, scales, tiles, arr((2, rows), F32)),
        [pltpu.VMEM((2, 2 * heads, GROUP), F32)],
        10**9,
    )
    sums = lax.all_gather(sums, "head")
    far_piece, ds, side_w, dout, delta = call(
        pieces_kernel,
        on(VMEM, q, side, scaled, side_lifted, side_scale, attended, sums),
        on(VMEM, rim, side_tiles, side_tiles, arr((2, heads, HDIM, GROUP), BF16), scales),
        [],
        10**9,
    )
    far_back = far_swap(far_piece)
    (near_piece,) = call(near_kernel, on(VMEM, q, side_w, ds, dout, fold), on(VMEM, packed), [sides], 10**9)
    near_back = near_swap(near_piece)
    own_tiles = pltpu.VMEM((2, heads, OWN, GROUP), BF16)
    own, mid_grad, spread, normed, query_grad = call(
        own_kernel,
        on(VMEM, q, k, v, mid, side, gain, lifted, own_scale, attended, sums, ds, dout, delta),
        on(VMEM, arr((2, rows, feats), F32), mids, arr((2, rows, 2 * SIDE + 2 * PACKED + rows // 4), BF16)) + on(HBM, whole, whole),
        [pltpu.VMEM((rows, feats), BF16), pltpu.VMEM((rows, feats), BF16), own_tiles, own_tiles, dma((4,))],
        10**6,
    )
    key_grad, value_grad = call(
        final_kernel,
        on(VMEM, own, mid_grad, spread, far_back, near_back),
        on(HBM, whole, whole),
        [pltpu.VMEM((rows, feats), BF16), pltpu.VMEM((rows, feats), BF16), dma((4,))],
        10**8,
    )
    return normed, query_grad, key_grad, value_grad


def solution(mesh):
    in_specs = (P("seq", "head"), P("seq", "head"), P("seq", "head"), P("head"), P("seq", "head"))
    out_specs = (P("seq", "head"), P("seq", "head"), P("seq", "head"), P("seq", "head"))
    return jax.shard_map(local, mesh=mesh, in_specs=in_specs, out_specs=out_specs, check_vma=False)
```

```python
import jax
import jax.numpy as jnp
from jax import lax
from jax.experimental import pallas as pl
from jax.experimental.pallas import tpu as pltpu
from jax.sharding import PartitionSpec as P

HEADS = 16
HDIM = 128
BLOCK = 16
SCALE = HDIM**-0.5
F32 = jnp.float32
BF16 = jnp.bfloat16

SIDE = 3 * BLOCK
RIM = SIDE + BLOCK
KEPT = BLOCK - 4
PACKED = BLOCK + 2 * KEPT
PARTS = 2
OWN_RAW = 9 * BLOCK
OWN_MID = 3 * BLOCK
OWN = OWN_RAW + OWN_MID
WINDOW = RIM + OWN
GROUP = 128


def dot(a, b, ca, cb):
    return lax.dot_general(a, b, (((ca,), (cb,)), ((), ())), preferred_element_type=F32)


def parity():
    return lax.axis_index("seq") % 2


def has_sides():
    index = lax.axis_index("seq")
    return (index > 0).astype(jnp.int32), (index < lax.axis_size("seq") - 1).astype(jnp.int32)


def iotas(shape):
    return lax.broadcasted_iota(jnp.int32, shape, 0), lax.broadcasted_iota(jnp.int32, shape, 1)


def one_if(flag, weight=1.0):
    return jnp.where(flag, weight, 0.0)


def pack_entries(p, row, rows, upper):
    middle = (1 - upper) * 4 + upper * (rows // 4 - BLOCK) - BLOCK
    coarse = (1 - upper) * 4 - BLOCK - KEPT
    raw_hit = one_if(p + upper * (rows - BLOCK) == row)
    mid_hit = one_if(p + middle == row // 4, 0.5)
    coarse_hit = one_if(p + coarse == row // 16, 0.25)
    return jnp.where(p < BLOCK, raw_hit, jnp.where(p < BLOCK + KEPT, mid_hit, coarse_hit))


def edge_entries(o, row, rows, upper):
    raw_hit = one_if(o + upper * (rows - BLOCK) == row)
    mid_hit = one_if(o - BLOCK + upper * (rows // 4 - BLOCK) == row // 4, 0.5)
    return jnp.where(o < BLOCK, raw_hit, jnp.where(o < 2 * BLOCK, mid_hit, one_if(o - 2 * BLOCK == row // 16, 0.25)))


def unpack_entries(o, n, upper):
    j, c = o - BLOCK, o - 2 * BLOCK
    from_raw = one_if((n < BLOCK) & (n // 4 == j - 12 * upper), 0.5)
    mid_hit = from_raw + one_if((n >= BLOCK) & (n < BLOCK + KEPT) & (n - BLOCK == j - 4 * (1 - upper)))
    coarse_hit = (
        one_if((n < BLOCK) & (c == 15 * upper), 0.25)
        + one_if((n >= BLOCK) & (n < BLOCK + KEPT) & ((n - BLOCK) // 4 == c - 1 - 11 * upper), 0.5)
        + one_if((n >= BLOCK + KEPT) & (n - BLOCK - KEPT == c - 4 * (1 - upper)))
    )
    return jnp.where(o < BLOCK, one_if(o == n), jnp.where(o < 2 * BLOCK, mid_hit, coarse_hit))


def unpack_both(o, n, upper):
    same = ((o >= SIDE) & (n >= PACKED)) | ((o < SIDE) & (n < PACKED))
    return jnp.where(same, unpack_entries(jnp.where(o >= SIDE, o - SIDE, o), jnp.where(n >= PACKED, n - PACKED, n), upper), 0.0)


def pack_kernel(k_hbm, v_hbm, k_ref, v_ref, far_ref, near_ref, mid_ref, sems):
    copies = [pltpu.make_async_copy(k_hbm, k_ref, sems.at[0]), pltpu.make_async_copy(v_hbm, v_ref, sems.at[1])]
    for copy in copies:
        copy.start()
    rows = k_ref.shape[0]
    mids = rows // 4
    upper = parity()
    out_row, row = iotas((mids, rows))
    parts = [one_if(out_row == row // 4, 0.5)]
    p, row = iotas((PACKED, rows))
    parts += [pack_entries(p, row, rows, edge) for edge in (upper, 1 - upper)]
    pool = jnp.concatenate(parts, axis=0).astype(BF16)
    pooled = []
    for i, ref in enumerate((k_ref, v_ref)):
        copies[i].wait()
        pooled.append(dot(pool, ref[...], 1, 0))
    for at, out_ref in ((mids, far_ref), (mids + PACKED, near_ref)):
        out_ref[...] = jnp.concatenate([x[at : at + PACKED] for x in pooled], axis=0).astype(BF16)
    for i in range(2):
        mid_ref[i] = pooled[i][:mids].astype(BF16)


def own_rows(i, g, cols, raw_ref, mid_ref):
    raw_at, mid_at = (g * (raw_ref.shape[0] - OWN_RAW), g * (mid_ref.shape[1] - OWN_MID))
    return [raw_ref[raw_at : raw_at + OWN_RAW, cols], mid_ref[i, mid_at : mid_at + OWN_MID, cols]]


def side_rows(i, g, cols, side_ref):
    base = i * SIDE
    return [side_ref[g, base : base + SIDE, cols], side_ref[1 - g, base + 2 * BLOCK : base + SIDE, cols]]


def window(i, g, cols, side_ref, raw_ref, mid_ref):
    return jnp.concatenate([*side_rows(i, g, cols, side_ref), *own_rows(i, g, cols, raw_ref, mid_ref)], axis=0)


def allowed(g, has_below, has_above):
    shape = (WINDOW, GROUP)
    kb = lax.broadcasted_iota(jnp.int32, shape, 0) // BLOCK
    qb = lax.broadcasted_iota(jnp.int32, shape, 1) // BLOCK
    qm = qb // 4
    raw_gap = kb - 4 - g - qb
    mid_gap = kb - 13 - g - qm
    edge_raw = qb == (7 if g else 0)
    edge_mid = qm == (1 if g else 0)
    one = jnp.ones(shape, jnp.int32)
    none = jnp.zeros(shape, jnp.int32)
    own = jnp.where(kb < 13, jnp.where(jnp.abs(raw_gap) <= 1, one, none), jnp.where(jnp.abs(mid_gap) == 1, one, none))
    side = jnp.where(kb == 0, jnp.where(edge_raw, one, none), jnp.where(kb == 1, jnp.where(edge_mid, one, none), one))
    valid_side, valid_other = (has_above, has_below) if g else (has_below, has_above)
    return jnp.where(kb < 3, side * valid_side, jnp.where(kb == 3, one * valid_other, own))


def local_kernel(
    k_ref, v_ref, mid_ref, q_hbm, cot_hbm, gain_hbm,
    q_ref, gain_ref, scaled_ref, lifted_ref, stats_ref, mix_ref, bias_ref, unfold_ref, fold_ref, spread_ref, cot_ref, own_bias, sems,
):
    copies = [
        pltpu.make_async_copy(src, dst, sems.at[n])
        for n, (src, dst) in enumerate([(q_hbm, q_ref), (cot_hbm, cot_ref), (gain_hbm, gain_ref)])
    ]
    for copy in copies:
        copy.start()
    for g in range(2):
        bias = jnp.where(allowed(g, *has_sides()) == 1, 0.0, -1e30)
        bias_ref[g] = bias[:RIM]
        own_bias[g] = bias[RIM:]
        unfold_ref[g] = unpack_both(*iotas((2 * SIDE, 2 * PACKED)), 1 - g).astype(BF16)
        fold_ref[g] = unpack_both(*iotas((2 * PACKED, 2 * SIDE))[::-1], 1 - g).astype(BF16)
    odd = parity()
    rows_all = q_ref.shape[0]
    row, p = iotas((rows_all, PACKED))
    near_part = pack_entries(p, row, rows_all, 1 - odd)
    row, o = iotas((rows_all, SIDE))
    far_part = edge_entries(o, row, rows_all, odd)
    no_near, no_far = jnp.zeros((rows_all, PACKED), F32), jnp.zeros((rows_all, SIDE), F32)
    row, at = iotas((rows_all, rows_all // 4))
    mid_part = one_if(row // 4 == at, 0.5)
    spread_ref[0] = jnp.concatenate([far_part, no_far, near_part, no_near, mid_part], axis=1).astype(BF16)
    spread_ref[1] = jnp.concatenate([no_far, far_part, no_near, near_part, mid_part], axis=1).astype(BF16)
    for copy in copies:
        copy.wait()
    heads = lifted_ref.shape[1]
    for g in range(2):
        rows = slice(g * GROUP, (g + 1) * GROUP)
        for h in range(heads):
            cols = slice(h * HDIM, (h + 1) * HDIM)
            keys = jnp.concatenate(own_rows(0, g, cols, k_ref, mid_ref), axis=0)
            scores = dot(keys, q_ref[rows, cols], 1, 1) * SCALE + own_bias[g]
            highest = jnp.max(scores, axis=0, keepdims=True)
            lifted = jnp.exp(scores - highest).astype(BF16)
            lifted_ref[g, h] = lifted
            stats_ref[g, h : h + 1] = highest
            stats_ref[g, heads + h : heads + h + 1] = jnp.sum(lifted.astype(F32), axis=0, keepdims=True)
            scaled_ref[g, h] = (cot_ref[rows, cols].astype(F32) * gain_ref[:, cols]).T
    for g in range(2):
        for h in range(heads):
            values = jnp.concatenate(own_rows(1, g, slice(h * HDIM, (h + 1) * HDIM), v_ref, mid_ref), axis=0)
            mix_ref[g, h] = dot(values, lifted_ref[g, h], 0, 0)


def forward_kernel(
    q_ref, far_ref, near_ref, bias_ref, unfold_ref, scaled_ref, stats_ref, mix_ref,
    side_ref, side_lifted, own_scale, side_scale, att_ref, sums_ref, side_stats,
):
    odd = parity()
    side_ref[odd] = dot(unfold_ref[odd], far_ref[...], 1, 0).astype(BF16)
    side_ref[1 - odd] = dot(unfold_ref[1 - odd], near_ref[...], 1, 0).astype(BF16)
    heads = mix_ref.shape[1]
    for g in range(2):
        rows = slice(g * GROUP, (g + 1) * GROUP)
        for h in range(heads):
            cols = slice(h * HDIM, (h + 1) * HDIM)
            keys = jnp.concatenate(side_rows(0, g, cols, side_ref), axis=0)
            scores = dot(keys, q_ref[rows, cols], 1, 1) * SCALE + bias_ref[g]
            highest = jnp.max(scores, axis=0, keepdims=True)
            lifted = jnp.exp(scores - highest).astype(BF16)
            side_lifted[g, h] = lifted
            side_stats[g, h : h + 1] = highest
            side_stats[g, heads + h : heads + h + 1] = jnp.sum(lifted.astype(F32), axis=0, keepdims=True)
    for g in range(2):
        rows = slice(g * GROUP, (g + 1) * GROUP)
        own_high, side_high = stats_ref[g, :heads], side_stats[g, :heads]
        highest = jnp.maximum(own_high, side_high)
        own_part, side_part = jnp.exp(own_high - highest), jnp.exp(side_high - highest)
        inverse = 1.0 / (stats_ref[g, heads:] * own_part + side_stats[g, heads:] * side_part)
        own_part, side_part = own_part * inverse, side_part * inverse
        own_scale[g] = own_part
        side_scale[g] = side_part
        squares = jnp.zeros((HDIM, GROUP), F32)
        crossed = jnp.zeros((HDIM, GROUP), F32)
        for h in range(heads):
            cols = slice(h * HDIM, (h + 1) * HDIM)
            values = jnp.concatenate(side_rows(1, g, cols, side_ref), axis=0)
            mixed = mix_ref[g, h] * own_part[h : h + 1] + dot(values, side_lifted[g, h], 0, 0) * side_part[h : h + 1]
            att_ref[g, h] = mixed
            squares += mixed * mixed
            crossed += mixed * scaled_ref[g, h]
        sums_ref[0:1, rows] = jnp.sum(squares, axis=0, keepdims=True)
        sums_ref[1:2, rows] = jnp.sum(crossed, axis=0, keepdims=True)


def row_factors(sums_ref):
    feat_all = HEADS * HDIM
    totals = sums_ref[0] + sums_ref[1]
    factor = lax.rsqrt(totals[0:1] / feat_all + 1e-06)
    return factor, factor * factor * factor * totals[1:2] / feat_all


def side_piece(g, q_ref, side_w, ds_ref, dout_ref, out_ref):
    half = q_ref.shape[0] // 2
    mine = pl.ds(pl.multiple_of(g * half, half), half)
    other = pl.ds(pl.multiple_of((1 - g) * half, half), half)
    blank = jnp.zeros((2 * BLOCK, GROUP), BF16)
    for h in range(side_w.shape[1]):
        cols = slice(h * HDIM, (h + 1) * HDIM)
        lefts = [
            jnp.concatenate([ref[g, h, :SIDE], jnp.concatenate([blank, ref[1 - g, h, SIDE:RIM]], axis=0)], axis=1)
            for ref in (ds_ref, side_w)
        ]
        queries = jnp.concatenate([q_ref[mine, cols], q_ref[other, cols]], axis=0)
        out_ref[:SIDE, cols] = dot(lefts[0], queries, 1, 0).astype(BF16)
        douts = jnp.concatenate([dout_ref[g, h], dout_ref[1 - g, h]], axis=1)
        out_ref[SIDE:, cols] = dot(lefts[1], douts, 1, 1).astype(BF16)


def pieces_kernel(
    q_ref, side_ref, scaled_ref, side_lifted, side_scale, att_ref, sums_ref,
    far_out, ds_ref, side_w, dout_ref, delta_ref,
):
    factor, cross = row_factors(sums_ref)
    heads = side_w.shape[1]
    for h in range(heads):
        cols = slice(h * HDIM, (h + 1) * HDIM)
        for g in range(2):
            rows = slice(g * GROUP, (g + 1) * GROUP)
            attended = att_ref[g, h]
            grad_out = (factor[:, rows] * scaled_ref[g, h] - cross[:, rows] * attended).astype(BF16)
            dout_ref[g, h] = grad_out
            delta = jnp.sum(grad_out.astype(F32) * attended, axis=0, keepdims=True)
            delta_ref[g, h : h + 1] = delta
            values = jnp.concatenate(side_rows(1, g, cols, side_ref), axis=0)
            weights = side_lifted[g, h].astype(F32) * side_scale[g, h : h + 1]
            side_w[g, h] = weights.astype(BF16)
            ds_ref[g, h] = (weights * (dot(values, grad_out, 1, 0) - delta) * SCALE).astype(BF16)
    side_piece(parity(), q_ref, side_w, ds_ref, dout_ref, far_out)


def near_kernel(q_ref, side_w, ds_ref, dout_ref, fold_ref, near_out, piece_ref):
    side = 1 - parity()
    side_piece(side, q_ref, side_w, ds_ref, dout_ref, piece_ref)
    near_out[...] = dot(fold_ref[side], piece_ref[...], 1, 0).astype(BF16)


def own_kernel(
    q_ref, k_ref, v_ref, mid_ref, side_ref, gain_ref, lifted_ref, own_scale, att_ref, sums_ref, ds_ref, dout_ref, delta_ref,
    own_ref, mid_grad, normed_hbm, dq_hbm, normed_ref, dq_ref, own_w, own_ds, sems,
):
    rows_all = q_ref.shape[0]
    heads = lifted_ref.shape[1]
    for h in range(heads):
        cols = slice(h * HDIM, (h + 1) * HDIM)
        for g in range(2):
            values = jnp.concatenate(own_rows(1, g, cols, v_ref, mid_ref), axis=0)
            weights = lifted_ref[g, h].astype(F32) * own_scale[g, h : h + 1]
            own_w[g, h] = weights.astype(BF16)
            own_ds[g, h] = (weights * (dot(values, dout_ref[g, h], 1, 0) - delta_ref[g, h : h + 1]) * SCALE).astype(BF16)
    factor, _ = row_factors(sums_ref)
    copies = []
    half = heads // 2
    for h in range(heads):
        cols = slice(h * HDIM, (h + 1) * HDIM)
        for g in range(2):
            rows = slice(g * GROUP, (g + 1) * GROUP)
            normed_ref[rows, cols] = ((att_ref[g, h] * factor[:, rows]).T * gain_ref[:, cols]).astype(BF16)
            keys = window(0, g, cols, side_ref, k_ref, mid_ref)
            dq_ref[rows, cols] = dot(jnp.concatenate([ds_ref[g, h], own_ds[g, h]], axis=0), keys, 0, 0).astype(BF16)
        if h % half == half - 1:
            done = pl.ds((h + 1 - half) * HDIM, half * HDIM)
            for ref, hbm in ((normed_ref, normed_hbm), (dq_ref, dq_hbm)):
                copies.append(pltpu.make_async_copy(ref.at[:, done], hbm.at[:, done], sems.at[len(copies)]))
                copies[-1].start()
    both_raw = 2 * OWN_RAW - rows_all
    both_mid = 2 * OWN_MID - rows_all // 4
    for h in range(heads):
        cols = slice(h * HDIM, (h + 1) * HDIM)
        inner = []
        for g in range(2):
            rows = slice(g * GROUP, (g + 1) * GROUP)
            inner.append((dot(own_ds[g, h], q_ref[rows, cols], 1, 0), dot(own_w[g, h], dout_ref[g, h], 1, 1)))
        for i in range(2):
            lower, upper = inner[0][i], inner[1][i]
            own_ref[i, :, cols] = jnp.concatenate(
                [lower[: OWN_RAW - both_raw], lower[OWN_RAW - both_raw : OWN_RAW] + upper[:both_raw], upper[both_raw:OWN_RAW]],
                axis=0,
            )
            low_mid, up_mid = lower[OWN_RAW:], upper[OWN_RAW:]
            mid_grad[i, :, cols] = jnp.concatenate(
                [low_mid[: OWN_MID - both_mid], low_mid[OWN_MID - both_mid :] + up_mid[:both_mid], up_mid[both_mid:]], axis=0
            ).astype(BF16)
    for copy in copies:
        copy.wait()


def final_kernel(own_ref, mid_grad, spread_ref, far_ref, near_ref, dk_hbm, dv_hbm, dk_ref, dv_ref, sems):
    width = own_ref.shape[2] // PARTS
    copies = []
    for i, (out_ref, hbm) in enumerate(((dk_ref, dk_hbm), (dv_ref, dv_hbm))):
        for part in range(PARTS):
            at = slice(part * width, (part + 1) * width)
            got = jnp.concatenate([far_ref[:, at], near_ref[:, at], mid_grad[i, :, at]], axis=0)
            out_ref[:, at] = (own_ref[i, :, at] + dot(spread_ref[i], got, 1, 0)).astype(BF16)
            copies.append(pltpu.make_async_copy(out_ref.at[:, at], hbm.at[:, at], sems.at[len(copies)]))
            copies[-1].start()
    for copy in copies:
        copy.wait()


VMEM = pl.BlockSpec(memory_space=pltpu.VMEM)
HBM = pl.BlockSpec(memory_space=pltpu.HBM)


def call(kernel, args, outs, scratch, flops):
    placed = [pltpu.with_memory_space_constraint(x, pltpu.HBM) if space is HBM else x for x, space in args]
    return pl.pallas_call(
        kernel,
        out_shape=tuple(shape for shape, _ in outs),
        in_specs=[space for _, space in args],
        out_specs=tuple(space for _, space in outs),
        scratch_shapes=scratch,
        compiler_params=pltpu.CompilerParams(vmem_limit_bytes=24 * 2**20),
        cost_estimate=pl.CostEstimate(flops=flops, bytes_accessed=flops // 256, transcendentals=0),
    )(*placed)


def on(space, *xs):
    return [(x, space) for x in xs]


def far_swap(x):
    pairs = [(i, i + 1) for i in range(1, lax.axis_size("seq") - 1, 2)]
    return lax.ppermute(x, "seq", pairs + [(j, i) for i, j in pairs])


def near_swap(x):
    pairs = [(i, i + 1) for i in range(0, lax.axis_size("seq"), 2)]
    return lax.ppermute(x, "seq", pairs + [(j, i) for i, j in pairs])


def local(queries, key_vectors, value_vectors, norm_gain, cotangent):
    rows, feats = queries.shape
    heads = feats // HDIM
    gain = norm_gain.reshape(1, feats)
    arr = jax.ShapeDtypeStruct
    dma = pltpu.SemaphoreType.DMA
    whole = arr((rows, feats), BF16)
    packed = arr((2 * PACKED, feats), BF16)
    mids = arr((2, rows // 4, feats), BF16)
    sides = pltpu.VMEM((2 * SIDE, feats), BF16)
    tiles = arr((2, heads, HDIM, GROUP), F32)
    k, v, far, near, mid = call(
        pack_kernel,
        on(HBM, key_vectors, value_vectors),
        on(VMEM, whole, whole, packed, packed, mids),
        [dma((2,))],
        10**8,
    )
    far_got = far_swap(far)
    near_got = near_swap(near)
    q, gain, scaled, lifted, stats, mix, bias, unfold, fold, spread = call(
        local_kernel,
        on(VMEM, k, v, mid) + on(HBM, queries, cotangent, gain),
        on(
            VMEM, whole, arr((1, feats), F32), tiles, arr((2, heads, OWN, GROUP), BF16), arr((2, 2 * heads, GROUP), F32),
            tiles, arr((2, RIM, GROUP), F32), arr((2, 2 * SIDE, 2 * PACKED), BF16), arr((2, 2 * PACKED, 2 * SIDE), BF16),
            arr((2, rows, 2 * SIDE + 2 * PACKED + rows // 4), BF16),
        ),
        [pltpu.VMEM((rows, feats), BF16), pltpu.VMEM((2, OWN, GROUP), F32), dma((3,))],
        10**9,
    )
    scales = arr((2, heads, GROUP), F32)
    side_tiles = arr((2, heads, RIM, GROUP), BF16)
    rim = arr((2 * SIDE, feats), BF16)
    side, side_lifted, own_scale, side_scale, attended, sums = call(
        forward_kernel,
        on(VMEM, q, far_got, near_got, bias, unfold, scaled, stats, mix),
        on(VMEM, arr((2, 2 * SIDE, feats), BF16), side_tiles, scales, scales, tiles, arr((2, rows), F32)),
        [pltpu.VMEM((2, 2 * heads, GROUP), F32)],
        10**9,
    )
    sums = lax.all_gather(sums, "head")
    far_piece, ds, side_w, dout, delta = call(
        pieces_kernel,
        on(VMEM, q, side, scaled, side_lifted, side_scale, attended, sums),
        on(VMEM, rim, side_tiles, side_tiles, arr((2, heads, HDIM, GROUP), BF16), scales),
        [],
        10**9,
    )
    far_back = far_swap(far_piece)
    (near_piece,) = call(near_kernel, on(VMEM, q, side_w, ds, dout, fold), on(VMEM, packed), [sides], 10**9)
    near_back = near_swap(near_piece)
    own_tiles = pltpu.VMEM((2, heads, OWN, GROUP), BF16)
    own, mid_grad, normed, query_grad = call(
        own_kernel,
        on(VMEM, q, k, v, mid, side, gain, lifted, own_scale, attended, sums, ds, dout, delta),
        on(VMEM, arr((2, rows, feats), F32), mids) + on(HBM, whole, whole),
        [pltpu.VMEM((rows, feats), BF16), pltpu.VMEM((rows, feats), BF16), own_tiles, own_tiles, dma((4,))],
        10**6,
    )
    key_grad, value_grad = call(
        final_kernel,
        on(VMEM, own, mid_grad, spread, far_back, near_back),
        on(HBM, whole, whole),
        [pltpu.VMEM((rows, feats), BF16), pltpu.VMEM((rows, feats), BF16), dma((2 * PARTS,))],
        10**8,
    )
    return normed, query_grad, key_grad, value_grad


def solution(mesh):
    in_specs = (P("seq", "head"), P("seq", "head"), P("seq", "head"), P("head"), P("seq", "head"))
    out_specs = (P("seq", "head"), P("seq", "head"), P("seq", "head"), P("seq", "head"))
    return jax.shard_map(local, mesh=mesh, in_specs=in_specs, out_specs=out_specs, check_vma=False)
```
